32 devices in a mesh: seq: 8 (over z, x), head: 4 (over y, core).
Axes of the slice: x: 2, y: 2, z: 4, core: 2. Of those that a mesh axis runs over, the one named last changes fastest.
Arguments:
- vis_in: bfloat16 [8, 256, 1280], P('seq'), may hold values from -6 to 6
- live_tiles: int32 [8], P('seq'), may hold values from 1 to 4
- ln1_gain: float32 [1280], replicated, may hold values from 0.5 to 1.5
- w_qkv: bfloat16 [3, 1280, 1280], P(None, None, 'head'), may hold values from -0.15625 to 0.15625
- w_out: bfloat16 [1280, 1280], P('head'), may hold values from -0.15625 to 0.15625
- ln2_gain: float32 [1280], replicated, may hold values from 0.5 to 1.5
- w_fc1: bfloat16 [1280, 5120], P(None, 'head'), may hold values from -0.15625 to 0.15625
- w_fc2: bfloat16 [5120, 1280], P('head'), may hold values from -0.078125 to 0.078125
- w_kv: bfloat16 [1280, 2, 1024], replicated, may hold values from -0.15625 to 0.15625
- k_gain: float32 [128], replicated, may hold values from 0.5 to 1.5
- q_gain: float32 [128], replicated, may hold values from 0.5 to 1.5
- text_queries: bfloat16 [2048, 8192], P('seq', 'head'), may hold values from -6 to 6
- block_mask: int32 [16, 8], P('seq'), may hold values from 0 to 1, as said below
Outputs:
- attended: bfloat16 [2048, 8192], P('seq', 'head')
The draws below stay inside these ranges and needn't reach their ends.
Inputs may be any that keep to these rules, and one draw needn't show every extreme that they name: `block_mask`: some blocks of text tokens attend to no image.
All inputs are finite; a program needn't handle non-finite values.
Results may differ from the reference program's by a relative error of at most 0.0085.
Values may be sent and summed in bfloat16 or wider, within the bound.
No kernel may reach another device: no remote copies, remote signals or barrier semaphores. Data moves between devices by JAX's collectives and lax.ppermute only.
A program may use at most 128 MiB of HBM per device.

```python
import math
import jax
import jax.numpy as jnp
from jax import lax

VIS = 1280
VHEADS = 16
VFF = 5120
QH = 64
KVH = 8
HD = 128
TILE_TOK = 64
QB = 128
VHD = 80
KI = 256
IMAGES = 8
TEXT = 2048


def draw_block_mask(key, part):
    key = jax.random.fold_in(key, 11)
    entry_key, block_key, forced_key = jax.random.split(key, 3)
    block_rows = TEXT // QB
    entries = jax.random.randint(entry_key, (block_rows, IMAGES), 0, 3) == 0
    silent = jax.random.randint(block_key, (block_rows, 1), 0, 8) == 0
    forced = jax.random.randint(forced_key, (), 0, block_rows)
    silent = silent | (jnp.arange(block_rows, dtype=jnp.int32)[:, None] == forced)
    return jnp.where(silent, 0, entries.astype(jnp.int32)).astype(jnp.int32)


def set_ends(array, own_key, smallest, largest):
    spot = [jax.random.randint(jax.random.fold_in(own_key, axis), (), 0, length) for axis, length in enumerate(array.shape)]
    main_axis = array.shape.index(max(array.shape))
    neighbour = spot[:main_axis] + [(spot[main_axis] + 1) % array.shape[main_axis]] + spot[main_axis + 1:]
    return array.at[tuple(spot)].set(smallest).at[tuple(neighbour)].set(largest)


def block_levels(own_key, dims, cuts, smallest, high):
    factor_of = 1.0
    for dim, parts in cuts:
        heights = jax.random.uniform(jax.random.fold_in(jax.random.fold_in(own_key, 6), dim), (parts,), jnp.float32, smallest / len(cuts), high / len(cuts))
        factor_of = factor_of * jnp.repeat(jnp.exp(heights), dims[dim] // parts).reshape((-1,) + (1,) * (len(dims) - 1 - dim))
    return factor_of


def scatter_about(key, shape, scale, limit, cuts=(), held_as=jnp.bfloat16):
    factor_of = block_levels(key, shape, cuts, -0.22, 0.18) if cuts else 1.0
    array = jax.random.normal(key, shape, jnp.float32) * scale * factor_of
    return jnp.minimum(jnp.maximum(array, -limit), limit).astype(held_as)


def setup_inputs(seed: int = 0) -> dict:
    key_list = jax.random.split(jax.random.key(seed), 14)
    return {
        "vis_in": scatter_about(key_list[0], (IMAGES, KI, VIS), 1.0, 6.0, ((0, 8),)),
        "live_tiles": set_ends(jax.random.randint(key_list[1], (IMAGES,), 1, 5), jax.random.fold_in(key_list[1], 1), 1, 4).astype(jnp.int32),
        "ln1_gain": jnp.clip(1.0 + 0.1 * jax.random.normal(key_list[2], (VIS,), jnp.float32), 0.5, 1.5),
        "w_qkv": scatter_about(key_list[3], (3, VIS, VIS), VIS ** -0.5, 0.15625, ((2, 4),)),
        "w_out": scatter_about(key_list[4], (VIS, VIS), VIS ** -0.5, 0.15625, ((0, 4),)),
        "ln2_gain": jnp.clip(1.0 + 0.1 * jax.random.normal(key_list[5], (VIS,), jnp.float32), 0.5, 1.5),
        "w_fc1": scatter_about(key_list[6], (VIS, VFF), VIS ** -0.5, 0.15625, ((1, 4),)),
        "w_fc2": scatter_about(key_list[7], (VFF, VIS), VFF ** -0.5, 0.078125, ((0, 4),)),
        "w_kv": scatter_about(key_list[8], (VIS, 2, KVH * HD), VIS ** -0.5, 0.15625),
        "k_gain": jnp.clip(1.0 + 0.1 * jax.random.normal(key_list[9], (HD,), jnp.float32), 0.5, 1.5),
        "q_gain": jnp.clip(1.0 + 0.1 * jax.random.normal(key_list[10], (HD,), jnp.float32), 0.5, 1.5),
        "text_queries": scatter_about(key_list[11], (TEXT, QH * HD), 1.0, 6.0, ((0, 8), (1, 4))),
        "block_mask": draw_block_mask(jax.random.fold_in(key_list[13], 71), 0),
    }


def layer_norm(values, gain):
    center = values - lax.optimization_barrier(jnp.mean(values, axis=-1, keepdims=True))
    spread = lax.optimization_barrier(jnp.mean(center * center, axis=-1, keepdims=True))
    return center / jnp.sqrt(spread + 1e-05) * gain

def rms_norm(values, gain):
    return values / jnp.sqrt(lax.optimization_barrier(jnp.mean(values * values, axis=-1, keepdims=True)) + 1e-05) * gain

def reference(vis_in, live_tiles, ln1_gain, w_qkv, w_out, ln2_gain, w_fc1, w_fc2, w_kv, k_gain, q_gain, text_queries, block_mask):
    all_rows = IMAGES * KI
    hidden_in = vis_in.astype(jnp.float32).reshape(all_rows, VIS)
    normed = layer_norm(hidden_in, ln1_gain).astype(jnp.bfloat16)
    projected = [jnp.dot(normed, w_qkv[which], preferred_element_type=jnp.float32).astype(jnp.bfloat16).reshape(IMAGES, KI, VHEADS, VHD) for which in range(3)]
    tile_of = jnp.arange(KI, dtype=jnp.int32) // TILE_TOK
    live = (tile_of[None, :] < live_tiles[:, None]).astype(jnp.float32)
    scores = jnp.einsum('iqhd,ikhd->ihqk', projected[0].astype(jnp.float32), projected[1].astype(jnp.float32)) / math.sqrt(VHD)
    expo = jnp.exp(scores) * live[:, None, None, :]
    probs = (expo / lax.optimization_barrier(jnp.sum(expo, axis=-1, keepdims=True))).astype(jnp.bfloat16)
    mixed = jnp.einsum('ihqk,ikhd->iqhd', probs.astype(jnp.float32), projected[2].astype(jnp.float32)).astype(jnp.bfloat16).reshape(all_rows, VIS)
    resid = hidden_in + jnp.dot(mixed, w_out, preferred_element_type=jnp.float32)
    normed2 = layer_norm(resid, ln2_gain).astype(jnp.bfloat16)
    inner = jax.nn.gelu(jnp.dot(normed2, w_fc1, preferred_element_type=jnp.float32), approximate=False).astype(jnp.bfloat16)
    vision_out = (resid + jnp.dot(inner, w_fc2, preferred_element_type=jnp.float32)).astype(jnp.bfloat16)
    key_value = jnp.dot(vision_out, w_kv.reshape(VIS, 2 * KVH * HD), preferred_element_type=jnp.float32).reshape(IMAGES, KI, 2, KVH, HD)
    keys = rms_norm(key_value[:, :, 0], k_gain).astype(jnp.bfloat16)
    values = key_value[:, :, 1].astype(jnp.bfloat16)
    group_size = QH // KVH
    queries = (rms_norm(text_queries.astype(jnp.float32).reshape(TEXT, QH, HD), q_gain) / math.sqrt(HD)).astype(jnp.bfloat16)
    queries = queries.reshape(TEXT, KVH, group_size, HD)
    row_mask = jnp.repeat(block_mask, QB, axis=0)
    flag_rows = lax.optimization_barrier(jnp.sum(row_mask, axis=1)) > 0
    mask_columns = row_mask.astype(jnp.float32).T

    def one_head(operands):
        head_queries, head_keys, head_values = operands
        query_f = head_queries.astype(jnp.float32)

        def one_image(totals, image_ops):
            image_keys, image_values, image_live, image_mask = image_ops
            denom, accum = totals
            sims = jnp.einsum('tgd,kd->tgk', query_f, image_keys.astype(jnp.float32))
            expo2 = jnp.exp(sims) * (image_mask[:, None, None] * image_live[None, None, :])
            rounded = lax.optimization_barrier(expo2.astype(jnp.bfloat16))
            accum = accum + jnp.einsum('tgk,kd->tgd', rounded.astype(jnp.float32), image_values.astype(jnp.float32))
            return ((denom + lax.optimization_barrier(jnp.sum(expo2, axis=-1)), accum), None)
        start = (jnp.zeros((TEXT, group_size), jnp.float32), jnp.zeros((TEXT, group_size, HD), jnp.float32))
        totals, _ = lax.scan(one_image, start, (head_keys, head_values, live, mask_columns))
        return totals
    denom, accum = lax.map(one_head, (queries.transpose(1, 0, 2, 3), keys.transpose(2, 0, 1, 3), values.transpose(2, 0, 1, 3)))
    safe = jnp.where(flag_rows[None, :, None], denom, jnp.float32(1.0))
    result = jnp.where(flag_rows[None, :, None, None], accum / safe[..., None], jnp.float32(0.0))
    return result.transpose(1, 0, 2, 3).reshape(TEXT, QH * HD).astype(jnp.bfloat16)
```

```python
import functools
import math

import jax
import jax.numpy as jnp
from jax import lax
from jax.experimental import pallas as pl
from jax.experimental.pallas import tpu as pltpu
from jax.sharding import PartitionSpec as P

KVH = 8
HD = 128
TILE_TOK = 64
QB = 128
VHD = 80
DEAD = 1e30
F32 = jnp.float32
BF16 = jnp.bfloat16

NT = (((1,), (1,)), ((), ()))
VM = pl.BlockSpec(memory_space=pltpu.VMEM)
SM = pl.BlockSpec(memory_space=pltpu.SMEM)


def params(mib):
    return pltpu.CompilerParams(vmem_limit_bytes=mib * 1024 * 1024)


def cost(flops, size, transcendentals=0):
    return pl.CostEstimate(flops=flops, bytes_accessed=size, transcendentals=transcendentals)


def layer_norm(values, gain):
    center = values - jnp.mean(values, axis=-1, keepdims=True)
    spread = jnp.mean(center * center, axis=-1, keepdims=True)
    return center / jnp.sqrt(spread + 1e-05) * gain


def rms_norm(values, gain):
    return values / jnp.sqrt(jnp.mean(values * values, axis=-1, keepdims=True) + 1e-05) * gain


def encode_kernel(core_ref, live_ref, x_ref, gain_ref, wqkv_ref, wout_ref, send_ref, keep_ref):
    rows = x_ref.shape[0]
    half = rows // 2
    normed = layer_norm(x_ref[...].astype(F32), gain_ref[...]).astype(BF16)
    q, k, v = [
        lax.dot_general(normed, wqkv_ref[j], NT, preferred_element_type=F32).astype(BF16)
        for j in range(3)
    ]
    width = q.shape[1]
    lane = lax.broadcasted_iota(jnp.int32, (1, width), 1)
    slot = lax.broadcasted_iota(jnp.int32, (1, rows), 1)
    live = jnp.where(slot < live_ref[0] * TILE_TOK, 1.0, 0.0).astype(F32)
    zero = jnp.zeros_like(q)
    mixed = jnp.zeros((rows, width), F32)
    for head in range(width // VHD):
        own = (lane >= head * VHD) & (lane < (head + 1) * VHD)
        scores = lax.dot_general(
            jnp.where(own, q, zero), k, NT, preferred_element_type=F32
        ) / math.sqrt(VHD)
        expo = jnp.exp(scores) * live
        probs = (expo / jnp.sum(expo, axis=-1, keepdims=True)).astype(BF16)
        mixed = mixed + jnp.dot(probs, jnp.where(own, v, zero), preferred_element_type=F32)
    keep_ref[...] = jnp.dot(mixed.astype(BF16), wout_ref[...], preferred_element_type=F32)
    core = core_ref[0]
    send_ref[...] = keep_ref[pl.ds(pl.multiple_of((1 - core) * half, half), half), :].astype(BF16)


def encode(core, live_tiles, x, gain, w_qkv_t, w_out):
    rows, width = x.shape
    own = w_out.shape[0]
    return pl.pallas_call(
        encode_kernel,
        in_specs=[SM, SM, VM, VM, VM, VM],
        out_specs=[VM, VM],
        out_shape=[
            jax.ShapeDtypeStruct((rows // 2, width), BF16),
            jax.ShapeDtypeStruct((rows, width), F32),
        ],
        compiler_params=params(32),
        cost_estimate=cost(2 * rows * width * 4 * own, 8 * width * own, rows * rows * own // VHD),
        name="encode",
    )(core, live_tiles, x, gain, w_qkv_t, w_out)


def mid_kernel(core_ref, x_ref, first_ref, second_ref, gain_ref, resid_ref, normed_ref):
    half = first_ref.shape[0]
    own = pl.ds(pl.multiple_of(core_ref[0] * half, half), half)
    resid = x_ref[own, :].astype(F32) + (first_ref[...].astype(F32) + second_ref[...].astype(F32))
    resid_ref[...] = resid
    normed_ref[...] = layer_norm(resid, gain_ref[...]).astype(BF16)


def mid(core, x, first, second, gain):
    half, width = first.shape
    return pl.pallas_call(
        mid_kernel,
        in_specs=[SM, VM, VM, VM, VM],
        out_specs=[VM, VM],
        out_shape=[
            jax.ShapeDtypeStruct((half, width), F32),
            jax.ShapeDtypeStruct((half, width), BF16),
        ],
        compiler_params=params(16),
        cost_estimate=cost(10 * half * width, 14 * half * width),
        name="mid",
    )(core, x, first, second, gain)


def mlp_kernel(own_ref, other_ref, w1_ref, w2_ref, send_ref, keep_ref):
    half = own_ref.shape[0]
    normed = jnp.concatenate([own_ref[...], other_ref[...]], axis=0)
    hidden = jnp.dot(normed, w1_ref[...], preferred_element_type=F32)
    inner = (0.5 * hidden * (1.0 + lax.erf(hidden * math.sqrt(0.5)))).astype(BF16)
    result = jnp.dot(inner, w2_ref[...], preferred_element_type=F32)
    keep_ref[...] = result[:half]
    send_ref[...] = result[half:].astype(BF16)


def mlp(own, other, w1, w2):
    half, width = own.shape
    return pl.pallas_call(
        mlp_kernel,
        in_specs=[VM, VM, VM, VM],
        out_specs=[VM, VM],
        out_shape=[
            jax.ShapeDtypeStruct((half, width), BF16),
            jax.ShapeDtypeStruct((half, width), F32),
        ],
        compiler_params=params(32),
        cost_estimate=cost(8 * half * w1.size, 4 * w1.size, 2 * half * w1.shape[1]),
        name="mlp",
    )(own, other, w1, w2)


def kv_kernel(
    core_ref, live_ref, resid_ref, first_ref, second_ref, w_ref, gain_ref, own_ref, send_ref, work
):
    half, width = resid_ref.shape
    block = own_ref.shape[1] // 2
    core = core_ref[0]
    vision = (
        resid_ref[...] + (first_ref[...].astype(F32) + second_ref[...].astype(F32))
    ).astype(BF16)
    work[...] = jnp.dot(vision, w_ref[...], preferred_element_type=F32)
    slot = lax.broadcasted_iota(jnp.int32, (half, 1), 0) + core * half
    live = slot < live_ref[0] * TILE_TOK
    gain = gain_ref[...]

    def write(ref, which):
        for head in range(block // HD):
            at = pl.multiple_of(which * block + head * HD, HD)
            keys = rms_norm(work[:, pl.ds(at, HD)], gain)
            ref[:, head * HD : (head + 1) * HD] = keys.astype(BF16)
            values = work[:, pl.ds(2 * block + at, HD)]
            ref[:, block + head * HD : block + (head + 1) * HD] = jnp.where(
                live, values, DEAD
            ).astype(BF16)

    write(send_ref, 1 - core)
    write(own_ref, core)


def project_kv(core, live_tiles, resid, first, second, w_chip, gain):
    half, width = resid.shape
    columns = w_chip.shape[1]
    return pl.pallas_call(
        kv_kernel,
        in_specs=[SM, SM, VM, VM, VM, VM, VM],
        out_specs=[VM, VM],
        out_shape=[jax.ShapeDtypeStruct((half, columns // 2), BF16)] * 2,
        scratch_shapes=[pltpu.VMEM((half, columns), F32)],
        compiler_params=params(24),
        cost_estimate=cost(2 * half * width * columns, 2 * width * columns),
        name="project_kv",
    )(core, live_tiles, resid, first, second, w_chip, gain)


def query_kernel(text_ref, gain_ref, out_ref):
    kv_local, blocks, rows, _ = out_ref.shape
    group = rows // QB
    gain = gain_ref[...]
    for head in range(kv_local):
        for block in range(blocks):
            for member in range(group):
                at = (head * group + member) * HD
                part = text_ref[block * QB : (block + 1) * QB, at : at + HD].astype(F32)
                out_ref[head, block, member * QB : (member + 1) * QB, :] = (
                    rms_norm(part, gain) / math.sqrt(HD)
                ).astype(BF16)


def norm_queries(text, gain, kv_local):
    rows, columns = text.shape
    group = columns // HD // kv_local
    return pl.pallas_call(
        query_kernel,
        in_specs=[VM, VM],
        out_specs=VM,
        out_shape=jax.ShapeDtypeStruct((kv_local, rows // QB, group * QB, HD), BF16),
        compiler_params=params(16),
        cost_estimate=cost(8 * rows * columns, 4 * rows * columns),
        name="norm_queries",
    )(text, gain)


def cross_kernel(slots, mask_ref, order_ref, q_ref, *refs):
    kv_refs, out_ref, acc, vals = refs[:slots], refs[slots], refs[slots + 1], refs[slots + 2]
    kv_local, blocks, rows, _ = q_ref.shape
    group = rows // QB
    images = mask_ref.shape[1]
    keys = kv_refs[0].shape[-2]
    acc[...] = jnp.zeros_like(acc)
    stacked = len(kv_refs) == 1

    def one_image(image, kv):
        for head in range(kv_local):
            values = kv[:, (kv_local + head) * HD : (kv_local + head + 1) * HD]
            live = values < DEAD * 0.5
            vals[:, :HD] = jnp.where(live, values, jnp.zeros_like(values))
            vals[:, HD:] = jnp.where(live, 1.0, 0.0).astype(BF16)
            for block in range(blocks):

                @pl.when(mask_ref[block, order_ref[image]] > 0)
                def _(head=head, block=block):
                    for member in range(group):
                        at = slice(member * QB, (member + 1) * QB)
                        sims = lax.dot_general(
                            q_ref[head, block, at, :],
                            kv[:, head * HD : (head + 1) * HD],
                            NT,
                            preferred_element_type=F32,
                        )
                        expo = jnp.exp(sims).astype(BF16)
                        acc[head, block, at, :] += jnp.dot(
                            expo, vals[...], preferred_element_type=F32
                        )

    if stacked:

        @pl.loop(0, images)
        def _(image):
            one_image(image, kv_refs[0].at[image])
    else:
        for image, kv in enumerate(kv_refs):
            one_image(image, kv)

    for block in range(blocks):
        seen = lax.fori_loop(
            0, images, lambda i, s, block=block: s + mask_ref[block, i], jnp.int32(0)
        )
        for head in range(kv_local):
            for member in range(group):
                at = slice(member * QB, (member + 1) * QB)
                total = acc[head, block, at, :HD]
                denom = acc[head, block, at, HD:]
                column = (head * group + member) * HD
                out_ref[block * QB : (block + 1) * QB, column : column + HD] = jnp.where(
                    seen > 0, total / jnp.where(seen > 0, denom, 1.0), 0.0
                ).astype(BF16)


def cross(mask, order, queries, kv_list):
    kv_local, blocks, rows, _ = queries.shape
    keys = kv_list[0].shape[-2]
    images = mask.shape[1]
    columns = kv_local * (rows // QB) * HD
    work = kv_local * blocks * rows * images * keys
    return pl.pallas_call(
        functools.partial(cross_kernel, len(kv_list)),
        in_specs=[SM, SM, VM] + [VM] * len(kv_list),
        out_specs=VM,
        out_shape=jax.ShapeDtypeStruct((blocks * QB, columns), BF16),
        scratch_shapes=[
            pltpu.VMEM((kv_local, blocks, rows, 2 * HD), F32),
            pltpu.VMEM((keys, 2 * HD), BF16),
        ],
        compiler_params=params(32),
        cost_estimate=cost(4 * work * HD, 4 * queries.size, work),
        name="cross",
    )(mask, order, queries, *kv_list)


def gather_line(block):
    def by(pairs):
        return functools.partial(lax.ppermute, axis_name="seq", perm=pairs)

    swap_x = by([(s, s ^ 1) for s in range(8)])
    swap_z = by([(s, s ^ 2) for s in range(8)])
    middle = by([(s, s ^ 6) for s in (2, 3, 4, 5)])
    outward = by([(2, 0), (3, 1), (4, 6), (5, 7)])
    seq = lax.axis_index("seq")
    z, x = seq // 2, seq % 2
    inside = (z == 1) | (z == 2)
    near = swap_z(block)
    side = swap_x(block)
    over = middle(block)
    near_side = swap_x(near)
    far = jnp.where(inside, over, outward(over))
    over_near = middle(near)
    far_side = swap_x(far)
    last = jnp.where(inside, over_near, outward(over_near))
    last_side = swap_x(last)
    far_z = jnp.where(z < 2, 2, 1)
    last_z = jnp.where(z < 2, 3, 0)
    order = [2 * z + x, 2 * z + 1 - x]
    for at in (z ^ 1, far_z, last_z):
        order += [2 * at + x, 2 * at + 1 - x]
    return [block, side, near, near_side, far, far_side, last, last_side], jnp.stack(order)


def per_device(
    vis_in,
    live_tiles,
    ln1_gain,
    w_qkv,
    w_out,
    ln2_gain,
    w_fc1,
    w_fc2,
    w_kv,
    k_gain,
    q_gain,
    text_queries,
    block_mask,
):
    head_count = lax.axis_size("head")
    head_index = lax.axis_index("head")
    core = head_index % 2
    core_arg = core.astype(jnp.int32).reshape(1)
    kv_local = KVH // head_count
    swap_core = functools.partial(
        lax.ppermute, axis_name="head", perm=[(i, i ^ 1) for i in range(head_count)]
    )

    def swap_chip(value, bit):
        return lax.ppermute(value, "head", [(i, i ^ bit) for i in range(head_count)])

    def sum_chips(value):
        bit = 2
        other = swap_chip(value, bit)
        while 2 * bit < head_count:
            bit *= 2
            value = (value.astype(F32) + other.astype(F32)).astype(BF16)
            other = swap_chip(value, bit)
        return value, other

    x = vis_in.reshape(vis_in.shape[0] * vis_in.shape[1], vis_in.shape[2])
    rows, width = x.shape
    half = rows // 2

    send, partial = encode(
        core_arg, live_tiles, x, ln1_gain.reshape(1, -1), jnp.swapaxes(w_qkv, 1, 2), w_out
    )
    kept = lax.dynamic_slice_in_dim(partial, core * half, half, 0)
    first, second = sum_chips((kept + swap_core(send).astype(F32)).astype(BF16))
    resid, normed = mid(core_arg, x, first, second, ln2_gain.reshape(1, -1))
    send, kept = mlp(normed, swap_core(normed), w_fc1, w_fc2)
    first, second = sum_chips((kept + swap_core(send).astype(F32)).astype(BF16))

    chip_columns = 2 * kv_local * HD
    w_chip = lax.dynamic_slice_in_dim(w_kv, (head_index // 2) * chip_columns, chip_columns, 2)
    w_chip = jnp.concatenate([w_chip[:, 0], w_chip[:, 1]], axis=1)
    own, send = project_kv(
        core_arg, live_tiles, resid, first, second, w_chip, k_gain.reshape(1, -1)
    )
    kv = jnp.concatenate([own, swap_core(send)], axis=0)

    queries = norm_queries(text_queries, q_gain.reshape(1, -1), kv_local)
    if lax.axis_size("seq") == 8:
        kv_list, order = gather_line(kv)
    else:
        kv_list = [lax.all_gather(kv, "seq", axis=0)]
        order = jnp.arange(block_mask.shape[1], dtype=jnp.int32)
    return cross(block_mask, order, queries, kv_list)


def solution(mesh):
    placed = (
        P("seq", None, None),
        P("seq"),
        P(),
        P(None, None, "head"),
        P("head", None),
        P(),
        P(None, "head"),
        P("head", None),
        P(),
        P(),
        P(),
        P("seq", "head"),
        P("seq", None),
    )
    return jax.shard_map(
        per_device, mesh=mesh, in_specs=placed, out_specs=P("seq", "head"), check_vma=False
    )
```

```python
import functools
import math

import jax
import jax.numpy as jnp
from jax import lax
from jax.experimental import pallas as pl
from jax.experimental.pallas import tpu as pltpu
from jax.sharding import PartitionSpec as P

KVH = 8
HD = 128
TILE_TOK = 64
QB = 128
VHD = 80
KI = 256
DEAD = 1e30
FIRST = 64
PARTS = [[0], [2, 1], [4, 3], [5, 6], [7]]
F32 = jnp.float32
BF16 = jnp.bfloat16

NT = (((1,), (1,)), ((), ()))
VM = pl.BlockSpec(memory_space=pltpu.VMEM)
SM = pl.BlockSpec(memory_space=pltpu.SMEM)
HB = pl.BlockSpec(memory_space=pltpu.HBM)
AN = pl.BlockSpec(memory_space=pl.ANY)


def params(mib):
    return pltpu.CompilerParams(vmem_limit_bytes=mib * 1024 * 1024)


def in_hbm(value):
    return pltpu.with_memory_space_constraint(value, pltpu.HBM)


def cost(flops, size, transcendentals=0):
    return pl.CostEstimate(flops=flops, bytes_accessed=size, transcendentals=transcendentals)


def layer_norm(values, gain):
    center = values - jnp.mean(values, axis=-1, keepdims=True)
    spread = jnp.mean(center * center, axis=-1, keepdims=True)
    return center / jnp.sqrt(spread + 1e-05) * gain


def rms_norm(values, gain):
    return values / jnp.sqrt(jnp.mean(values * values, axis=-1, keepdims=True) + 1e-05) * gain


def encode_kernel(
    core_ref,
    live_ref,
    gain_hbm,
    x_hbm,
    wqkv_hbm,
    wout_hbm,
    send_ref,
    keep_ref,
    own_ref,
    gain_ref,
    x_ref,
    wqkv_ref,
    wout_ref,
    mixed_ref,
    sems,
):
    loads = [pltpu.make_async_copy(x_hbm, x_ref, sems.at[0])]
    loads += [
        pltpu.make_async_copy(wqkv_hbm.at[j], wqkv_ref.at[j], sems.at[1 + j]) for j in range(3)
    ]
    loads.append(pltpu.make_async_copy(wout_hbm, wout_ref, sems.at[4]))
    loads.append(pltpu.make_async_copy(gain_hbm, gain_ref, sems.at[5]))
    for load in loads:
        load.start()
    rows, width = mixed_ref.shape
    half = rows // 2
    core = core_ref[0]
    own_rows = pl.ds(pl.multiple_of(core * half, half), half)
    other_rows = pl.ds(pl.multiple_of((1 - core) * half, half), half)

    loads[0].wait()
    loads[5].wait()
    own_ref[...] = x_ref[own_rows, :]
    normed = layer_norm(x_ref[...].astype(F32), gain_ref[...].reshape(1, -1)).astype(BF16)
    qkv = []
    for j in range(3):
        loads[1 + j].wait()
        qkv.append(
            lax.dot_general(normed, wqkv_ref[j], NT, preferred_element_type=F32).astype(BF16)
        )
    q, k, v = qkv
    lane = lax.broadcasted_iota(jnp.int32, (1, width), 1)
    slot = lax.broadcasted_iota(jnp.int32, (1, rows), 1)
    live = jnp.where(slot < live_ref[0] * TILE_TOK, 1.0, 0.0).astype(F32)
    zero = jnp.zeros_like(q)
    mixed = jnp.zeros((rows, width), F32)
    for head in range(width // VHD):
        own = (lane >= head * VHD) & (lane < (head + 1) * VHD)
        scores = lax.dot_general(
            jnp.where(own, q, zero), k, NT, preferred_element_type=F32
        ) / math.sqrt(VHD)
        expo = jnp.exp(scores) * live
        probs = (expo / jnp.sum(expo, axis=-1, keepdims=True)).astype(BF16)
        mixed = mixed + jnp.dot(probs, jnp.where(own, v, zero), preferred_element_type=F32)
    mixed_ref[...] = mixed.astype(BF16)
    loads[4].wait()
    send_ref[...] = jnp.dot(
        mixed_ref[other_rows, :], wout_ref[...], preferred_element_type=F32
    ).astype(BF16)
    keep_ref[...] = jnp.dot(mixed_ref[own_rows, :], wout_ref[...], preferred_element_type=F32)


def encode(core, live_tiles, x, gain, w_qkv_t, w_out):
    rows, width = x.shape
    own = w_out.shape[0]
    return pl.pallas_call(
        encode_kernel,
        in_specs=[SM, SM, HB, HB, HB, HB],
        out_specs=[VM, VM, VM],
        out_shape=[
            jax.ShapeDtypeStruct((rows // 2, width), BF16),
            jax.ShapeDtypeStruct((rows // 2, width), F32),
            jax.ShapeDtypeStruct((rows // 2, width), BF16),
        ],
        scratch_shapes=[
            pltpu.VMEM(gain.shape, F32),
            pltpu.VMEM(x.shape, BF16),
            pltpu.VMEM(w_qkv_t.shape, BF16),
            pltpu.VMEM(w_out.shape, BF16),
            pltpu.VMEM((rows, own), BF16),
            pltpu.SemaphoreType.DMA((6,)),
        ],
        compiler_params=params(12),
        cost_estimate=cost(2 * rows * width * 4 * own, 8 * width * own, rows * rows * own // VHD),
        name="encode",
    )(core, live_tiles, in_hbm(gain), in_hbm(x), in_hbm(w_qkv_t), in_hbm(w_out))


def mid_kernel(x_ref, first_ref, second_ref, gain_ref, _, resid_ref, normed_ref):
    resid = x_ref[...].astype(F32) + (first_ref[...].astype(F32) + second_ref[...].astype(F32))
    resid_ref[...] = resid
    normed_ref[...] = layer_norm(resid, gain_ref[...].reshape(1, -1)).astype(BF16)


def mid(x, first, second, gain, after):
    half, width = first.shape
    return pl.pallas_call(
        mid_kernel,
        in_specs=[VM, VM, VM, VM, AN],
        out_specs=[VM, VM],
        out_shape=[
            jax.ShapeDtypeStruct((half, width), F32),
            jax.ShapeDtypeStruct((half, width), BF16),
        ],
        compiler_params=params(8),
        cost_estimate=cost(10 * half * width, 14 * half * width),
        name="mid",
    )(x, first, second, gain, after)


def fetch_kernel(chip_ref, w1_hbm, w2_hbm, wkv_hbm, _, w1_ref, w2_ref, wkv_ref, sems):
    columns = wkv_ref.shape[2]
    mine = pl.ds(pl.multiple_of(chip_ref[0] * columns, HD), columns)
    loads = [
        pltpu.make_async_copy(w1_hbm, w1_ref, sems.at[0]),
        pltpu.make_async_copy(w2_hbm, w2_ref, sems.at[1]),
        pltpu.make_async_copy(wkv_hbm.at[:, :, mine], wkv_ref, sems.at[2]),
    ]
    for load in loads:
        load.start()
    for load in loads:
        load.wait()


def fetch(chip, w1, w2, w_kv, columns, after):
    shapes = [w1.shape, w2.shape, (w_kv.shape[0], w_kv.shape[1], columns)]
    return pl.pallas_call(
        fetch_kernel,
        in_specs=[SM, HB, HB, HB, AN],
        out_specs=[VM, VM, VM],
        out_shape=[jax.ShapeDtypeStruct(shape, BF16) for shape in shapes],
        scratch_shapes=[pltpu.SemaphoreType.DMA((3,))],
        compiler_params=params(16),
        cost_estimate=cost(0, 20 * w1.size),
        name="fetch",
    )(chip, in_hbm(w1), in_hbm(w2), in_hbm(w_kv), after)


def mlp_kernel(own_ref, other_ref, w1_ref, w2_ref, send_ref, keep_ref):
    half = own_ref.shape[0]
    normed = jnp.concatenate([own_ref[...], other_ref[...]], axis=0)
    hidden = jnp.dot(normed, w1_ref[...], preferred_element_type=F32)
    inner = (0.5 * hidden * (1.0 + lax.erf(hidden * math.sqrt(0.5)))).astype(BF16)
    result = jnp.dot(inner, w2_ref[...], preferred_element_type=F32)
    keep_ref[...] = result[:half]
    send_ref[...] = result[half:].astype(BF16)


def mlp(own, other, w1, w2):
    half, width = own.shape
    return pl.pallas_call(
        mlp_kernel,
        in_specs=[VM, VM, VM, VM],
        out_specs=[VM, VM],
        out_shape=[
            jax.ShapeDtypeStruct((half, width), BF16),
            jax.ShapeDtypeStruct((half, width), F32),
        ],
        compiler_params=params(14),
        cost_estimate=cost(8 * half * w1.size, 4 * w1.size, 2 * half * w1.shape[1]),
        name="mlp",
    )(own, other, w1, w2)


def kv_kernel(start, core_ref, live_ref, keys_ref, gain_ref, _, own_ref, send_ref):
    half = keys_ref.shape[1]
    block = own_ref.shape[1] // 2
    core = core_ref[0]
    slot = lax.broadcasted_iota(jnp.int32, (half, 1), 0) + core * (KI // 2) + start
    live = slot < live_ref[0] * TILE_TOK
    gain = gain_ref[...].reshape(1, -1)

    def write(ref, which):
        for head in range(block // HD):
            at = pl.ds(pl.multiple_of(which * block + head * HD, HD), HD)
            keys = rms_norm(keys_ref[0, :, at], gain)
            ref[:, head * HD : (head + 1) * HD] = keys.astype(BF16)
            values = keys_ref[1, :, at]
            ref[:, block + head * HD : block + (head + 1) * HD] = jnp.where(
                live, values, DEAD
            ).astype(BF16)

    write(send_ref, 1 - core)
    write(own_ref, core)


def finish_kv(start, core, live_tiles, key_value, gain, after):
    _, half, columns = key_value.shape
    return pl.pallas_call(
        functools.partial(kv_kernel, start),
        in_specs=[SM, SM, VM, VM, AN],
        out_specs=[VM, VM],
        out_shape=[jax.ShapeDtypeStruct((half, columns), BF16)] * 2,
        compiler_params=params(8),
        cost_estimate=cost(10 * key_value.size, 6 * key_value.size),
        name="finish_kv",
    )(core, live_tiles, key_value, gain, after)


def query_kernel(text_ref, gain_ref, out_ref):
    kv_local, blocks, rows, _ = out_ref.shape
    group = rows // QB
    gain = gain_ref[...].reshape(1, -1)
    for head in range(kv_local):
        for block in range(blocks):
            for member in range(group):
                at = (head * group + member) * HD
                part = text_ref[block * QB : (block + 1) * QB, at : at + HD].astype(F32)
                out_ref[head, block, member * QB : (member + 1) * QB, :] = (
                    rms_norm(part, gain) / math.sqrt(HD)
                ).astype(BF16)


def norm_queries(text, gain, kv_local):
    rows, columns = text.shape
    group = columns // HD // kv_local
    return pl.pallas_call(
        query_kernel,
        in_specs=[VM, VM],
        out_specs=VM,
        out_shape=jax.ShapeDtypeStruct((kv_local, rows // QB, group * QB, HD), BF16),
        compiler_params=params(8),
        cost_estimate=cost(8 * rows * columns, 4 * rows * columns),
        name="norm_queries",
    )(text, gain)


def cross_kernel(slots, first, last, mask_ref, seq_ref, q_ref, *refs):
    flat = sum(count for _, count in slots)
    kv_refs, refs = list(refs[:flat]), refs[flat:]
    refs = refs if first else refs[1:]
    out_ref, acc, vals = refs if last else (None, *refs)
    kv_local, blocks, rows, _ = q_ref.shape
    group = rows // QB
    images = mask_ref.shape[1]
    if first:
        acc[...] = jnp.zeros_like(acc)

    def one_image(image, chunks):
        for head in range(kv_local):
            at = 0
            for kv in chunks:
                values = kv[:, (kv_local + head) * HD : (kv_local + head + 1) * HD]
                live = values < DEAD * 0.5
                span = slice(at, at + values.shape[0])
                vals[head, span, :HD] = jnp.where(live, values, jnp.zeros_like(values))
                vals[head, span, HD:] = jnp.where(live, 1.0, 0.0).astype(BF16)
                at += values.shape[0]
        for block in range(blocks):

            @pl.when(mask_ref[block, image] > 0)
            def _(block=block):
                for head in range(kv_local):
                    keys = [kv[:, head * HD : (head + 1) * HD] for kv in chunks]
                    keys = keys[0] if len(keys) == 1 else jnp.concatenate(keys, axis=0)
                    for member in range(group):
                        at = slice(member * QB, (member + 1) * QB)
                        sims = lax.dot_general(
                            q_ref[head, block, at, :], keys, NT, preferred_element_type=F32
                        )
                        expo = jnp.exp(sims).astype(BF16)
                        acc[head, block, at, :] += jnp.dot(
                            expo, vals[head], preferred_element_type=F32
                        )

    if slots[0][0] is None:

        @pl.loop(0, images)
        def _(image):
            one_image(image, [kv_refs[0].at[image]])
    else:
        for bits, count in slots:
            one_image(seq_ref[0] ^ bits, [kv_refs.pop(0) for _ in range(count)])

    if not last:
        return
    for block in range(blocks):
        seen = lax.fori_loop(
            0, images, lambda i, s, block=block: s + mask_ref[block, i], jnp.int32(0)
        )
        for head in range(kv_local):
            for member in range(group):
                at = slice(member * QB, (member + 1) * QB)
                total = acc[head, block, at, :HD]
                denom = acc[head, block, at, HD:]
                column = (head * group + member) * HD
                out_ref[block * QB : (block + 1) * QB, column : column + HD] = jnp.where(
                    seen > 0, total / jnp.where(seen > 0, denom, 1.0), 0.0
                ).astype(BF16)


def cross(mask, seq, queries, slots, acc=None, last=True):
    kv_local, blocks, rows, _ = queries.shape
    flat = [chunk for _, chunks in slots for chunk in chunks]
    keys = sum(chunk.shape[-2] for chunk in slots[0][1])
    columns = kv_local * (rows // QB) * HD
    work = blocks * rows * sum(kv.size for kv in flat) // (2 * HD)
    sums = (kv_local, blocks, rows, 2 * HD)
    given = [] if acc is None else [acc]
    shapes = [jax.ShapeDtypeStruct((blocks * QB, columns), BF16)] * last
    shapes.append(jax.ShapeDtypeStruct(sums, F32))
    result = pl.pallas_call(
        functools.partial(
            cross_kernel, [(bits, len(chunks)) for bits, chunks in slots], acc is None, last
        ),
        in_specs=[SM, SM, VM] + [VM] * len(flat + given),
        out_specs=[VM] * len(shapes),
        out_shape=shapes,
        scratch_shapes=[pltpu.VMEM((kv_local, keys, 2 * HD), BF16)],
        input_output_aliases={3 + len(flat): len(shapes) - 1} if given else {},
        compiler_params=params(14),
        cost_estimate=cost(4 * work * HD, 4 * queries.size, work),
        name="cross",
    )(mask, seq, queries, *flat, *given)
    return result[0]


def swap_line(bits, value):
    return lax.ppermute(value, "seq", [(s, s ^ bits) for s in range(8)])


def tie(values, *after):
    return lax.optimization_barrier((tuple(values), after))[0]


def gather_line(blocks):
    images = []
    for block in blocks:
        images.append({0: block, 4: swap_line(4, block), 2: swap_line(2, block)})
    crossed = []

    def swap_x(value):
        if len(crossed) > 1:
            value = tie((value,), crossed[-2])[0]
        crossed.append(swap_line(1, value))
        return crossed[-1]

    for got in images:
        got[1] = swap_x(got[0])
    for got in images:
        got[3] = swap_x(got[2])
        got[6] = swap_line(2, tie((got[4],), got[2])[0])
        got[5] = swap_x(got[4])
    for number, got in enumerate(images):
        if number == len(images) - 1 and number > 0:
            got[7] = swap_line(2, got[5])
        else:
            got[7] = swap_x(got[6])
    return images


def per_device(
    vis_in,
    live_tiles,
    ln1_gain,
    w_qkv,
    w_out,
    ln2_gain,
    w_fc1,
    w_fc2,
    w_kv,
    k_gain,
    q_gain,
    text_queries,
    block_mask,
):
    head_count = lax.axis_size("head")
    head_index = lax.axis_index("head")
    core = head_index % 2
    core_arg = core.astype(jnp.int32).reshape(1)
    kv_local = KVH // head_count
    swap_core = functools.partial(
        lax.ppermute, axis_name="head", perm=[(i, i ^ 1) for i in range(head_count)]
    )

    def swap_chip(value, bit):
        return lax.ppermute(value, "head", [(i, i ^ bit) for i in range(head_count)])

    def sum_chips(value):
        bit = 2
        other = swap_chip(value, bit)
        while 2 * bit < head_count:
            bit *= 2
            value = (value.astype(F32) + other.astype(F32)).astype(BF16)
            other = swap_chip(value, bit)
        return value, other

    x = vis_in.reshape(vis_in.shape[0] * vis_in.shape[1], vis_in.shape[2])
    rows, width = x.shape
    half = rows // 2
    line = lax.axis_size("seq") == 8
    cuts = [0, half * FIRST // 128, half] if line else [0, half]
    chunks = [slice(at, end) for at, end in zip(cuts, cuts[1:])]
    chip_columns = 2 * kv_local * HD

    queries = norm_queries(text_queries, q_gain, kv_local)
    send, kept, own_x = encode(
        core_arg, live_tiles, x, ln1_gain, jnp.swapaxes(w_qkv, 1, 2), w_out
    )
    received = swap_core(send)
    chip_arg = (head_index // 2).astype(jnp.int32).reshape(1)
    first = (kept + received.astype(F32)).astype(BF16)
    w1, w2, w_chip = fetch(chip_arg, w_fc1, w_fc2, w_kv, chip_columns, first)
    first, second = sum_chips(first)
    resid, normed = mid(own_x, first, second, ln2_gain, w_chip)
    other = swap_core(normed)
    sums = []
    for at in chunks:
        send, keep = mlp(normed[at], other[at], w1, w2)
        sums.append((keep + swap_core(send).astype(F32)).astype(BF16))
    sums = [sum_chips(value) for value in sums]
    blocks = []
    for at, (first, second) in zip(chunks, sums):
        second = tie((second,), blocks[-1] if blocks else sums[-1][0])[0]
        vision = (resid[at] + (first.astype(F32) + second.astype(F32))).astype(BF16)
        key_value = jnp.einsum("rc,cjd->jrd", vision, w_chip, preferred_element_type=F32)
        own, send = finish_kv(at.start, core_arg, live_tiles, key_value, k_gain, queries)
        blocks.append(jnp.concatenate([own, swap_core(send)], axis=0))

    seq = lax.axis_index("seq").astype(jnp.int32).reshape(1)
    if not line:
        stacked = lax.all_gather(jnp.concatenate(blocks, axis=0), "seq", axis=0)
        return cross(block_mask, seq, queries, [(None, [stacked])])
    gathered = gather_line(blocks)
    acc = None
    for number, part in enumerate(PARTS):
        slots = [(bits, [images[bits] for images in gathered]) for bits in part]
        acc = cross(block_mask, seq, queries, slots, acc, number == len(PARTS) - 1)
    return acc


def solution(mesh):
    placed = (
        P("seq", None, None),
        P("seq"),
        P(),
        P(None, None, "head"),
        P("head", None),
        P(),
        P(None, "head"),
        P("head", None),
        P(),
        P(),
        P(),
        P("seq", "head"),
        P("seq", None),
    )
    return jax.shard_map(
        per_device, mesh=mesh, in_specs=placed, out_specs=P("seq", "head"), check_vma=False
    )
```

```python
import functools
import math

import jax
import jax.numpy as jnp
from jax import lax
from jax.experimental import pallas as pl
from jax.experimental.pallas import tpu as pltpu
from jax.sharding import PartitionSpec as P

KVH = 8
HD = 128
TILE_TOK = 64
QB = 128
VHD = 80
KI = 256
DEAD = 1e30
FIRST = 64
EARLY = [[0], [2, 1]]
LATE = [[4, 3], [5, 6], [7]]
F32 = jnp.float32
BF16 = jnp.bfloat16

NT = (((1,), (1,)), ((), ()))
VM = pl.BlockSpec(memory_space=pltpu.VMEM)
SM = pl.BlockSpec(memory_space=pltpu.SMEM)
HB = pl.BlockSpec(memory_space=pltpu.HBM)
AN = pl.BlockSpec(memory_space=pl.ANY)


def params(mib):
    return pltpu.CompilerParams(vmem_limit_bytes=mib * 1024 * 1024)


def in_hbm(value):
    return pltpu.with_memory_space_constraint(value, pltpu.HBM)


def cost(flops, size, transcendentals=0):
    return pl.CostEstimate(flops=flops, bytes_accessed=size, transcendentals=transcendentals)


def layer_norm(values, gain):
    center = values - jnp.mean(values, axis=-1, keepdims=True)
    spread = jnp.mean(center * center, axis=-1, keepdims=True)
    return center * (1.0 / jnp.sqrt(spread + 1e-05)) * gain


def rms_norm(values, gain):
    square = jnp.mean(values * values, axis=-1, keepdims=True)
    return values * (1.0 / jnp.sqrt(square + 1e-05)) * gain


def encode_kernel(
    core_ref,
    live_ref,
    gain_hbm,
    x_hbm,
    wqkv_hbm,
    wout_hbm,
    send_ref,
    keep_ref,
    own_ref,
    gain_ref,
    x_ref,
    wqkv_ref,
    wout_ref,
    mixed_ref,
    sems,
):
    loads = [pltpu.make_async_copy(x_hbm, x_ref, sems.at[0])]
    loads += [
        pltpu.make_async_copy(wqkv_hbm.at[j], wqkv_ref.at[j], sems.at[1 + j]) for j in range(3)
    ]
    loads.append(pltpu.make_async_copy(wout_hbm, wout_ref, sems.at[4]))
    loads.append(pltpu.make_async_copy(gain_hbm, gain_ref, sems.at[5]))
    for load in loads:
        load.start()
    rows, width = mixed_ref.shape
    half = rows // 2
    core = core_ref[0]
    own_rows = pl.ds(pl.multiple_of(core * half, half), half)
    other_rows = pl.ds(pl.multiple_of((1 - core) * half, half), half)

    loads[0].wait()
    loads[5].wait()
    own_ref[...] = x_ref[own_rows, :]
    normed = layer_norm(x_ref[...].astype(F32), gain_ref[...].reshape(1, -1)).astype(BF16)
    for load in loads[1:4]:
        load.wait()
    weights = wqkv_ref[...].reshape(3 * width, x_ref.shape[1])
    qkv = lax.dot_general(normed, weights, NT, preferred_element_type=F32).astype(BF16)
    q, k, v = [qkv[:, j * width : (j + 1) * width] for j in range(3)]
    lane = lax.broadcasted_iota(jnp.int32, (1, width), 1)
    slot = lax.broadcasted_iota(jnp.int32, (1, rows), 1)
    live = jnp.where(slot < live_ref[0] * TILE_TOK, 1.0, 0.0).astype(F32)
    zero = jnp.zeros_like(q)
    mixed = jnp.zeros((rows, width), F32)
    for head in range(width // VHD):
        own = (lane >= head * VHD) & (lane < (head + 1) * VHD)
        scores = lax.dot_general(jnp.where(own, q, zero), k, NT, preferred_element_type=F32)
        expo = jnp.exp(scores * (1.0 / math.sqrt(VHD))) * live
        probs = (expo * (1.0 / jnp.sum(expo, axis=-1, keepdims=True))).astype(BF16)
        mixed = mixed + jnp.dot(probs, jnp.where(own, v, zero), preferred_element_type=F32)
    mixed_ref[...] = mixed.astype(BF16)
    loads[4].wait()
    send_ref[...] = jnp.dot(
        mixed_ref[other_rows, :], wout_ref[...], preferred_element_type=F32
    ).astype(BF16)
    keep_ref[...] = jnp.dot(mixed_ref[own_rows, :], wout_ref[...], preferred_element_type=F32)


def encode(core, live_tiles, x, gain, w_qkv_t, w_out):
    rows, width = x.shape
    own = w_out.shape[0]
    return pl.pallas_call(
        encode_kernel,
        in_specs=[SM, SM, HB, HB, HB, HB],
        out_specs=[VM, VM, VM],
        out_shape=[
            jax.ShapeDtypeStruct((rows // 2, width), BF16),
            jax.ShapeDtypeStruct((rows // 2, width), F32),
            jax.ShapeDtypeStruct((rows // 2, width), BF16),
        ],
        scratch_shapes=[
            pltpu.VMEM(gain.shape, F32),
            pltpu.VMEM(x.shape, BF16),
            pltpu.VMEM(w_qkv_t.shape, BF16),
            pltpu.VMEM(w_out.shape, BF16),
            pltpu.VMEM((rows, own), BF16),
            pltpu.SemaphoreType.DMA((6,)),
        ],
        compiler_params=params(12),
        cost_estimate=cost(2 * rows * width * 4 * own, 8 * width * own, rows * rows * own // VHD),
        name="encode",
    )(core, live_tiles, in_hbm(gain), in_hbm(x), in_hbm(w_qkv_t), in_hbm(w_out))


def mid_kernel(x_ref, first_ref, second_ref, gain_ref, _, __, resid_ref, normed_ref):
    resid = x_ref[...].astype(F32) + (first_ref[...].astype(F32) + second_ref[...].astype(F32))
    resid_ref[...] = resid
    normed_ref[...] = layer_norm(resid, gain_ref[...].reshape(1, -1)).astype(BF16)


def mid(x, first, second, gain, *after):
    half, width = first.shape
    return pl.pallas_call(
        mid_kernel,
        in_specs=[VM, VM, VM, VM, AN, AN],
        out_specs=[VM, VM],
        out_shape=[
            jax.ShapeDtypeStruct((half, width), F32),
            jax.ShapeDtypeStruct((half, width), BF16),
        ],
        compiler_params=params(8),
        cost_estimate=cost(10 * half * width, 14 * half * width),
        name="mid",
    )(x, first, second, gain, *after)


def fetch_kernel(chip_ref, w1_hbm, w2_hbm, wkv_hbm, _, w1_ref, w2_ref, wkv_ref, sems):
    columns = wkv_ref.shape[2]
    mine = pl.ds(pl.multiple_of(chip_ref[0] * columns, HD), columns)
    loads = [
        pltpu.make_async_copy(w1_hbm, w1_ref, sems.at[0]),
        pltpu.make_async_copy(w2_hbm, w2_ref, sems.at[1]),
        pltpu.make_async_copy(wkv_hbm.at[:, :, mine], wkv_ref, sems.at[2]),
    ]
    for load in loads:
        load.start()
    for load in loads:
        load.wait()


def fetch(chip, w1, w2, w_kv, columns, after):
    shapes = [w1.shape, w2.shape, (w_kv.shape[0], w_kv.shape[1], columns)]
    return pl.pallas_call(
        fetch_kernel,
        in_specs=[SM, HB, HB, HB, AN],
        out_specs=[VM, VM, VM],
        out_shape=[jax.ShapeDtypeStruct(shape, BF16) for shape in shapes],
        scratch_shapes=[pltpu.SemaphoreType.DMA((3,))],
        compiler_params=params(16),
        cost_estimate=cost(0, 20 * w1.size),
        name="fetch",
    )(chip, in_hbm(w1), in_hbm(w2), in_hbm(w_kv), after)


def mlp_kernel(normed_ref, w1_ref, w2_ref, out_ref):
    hidden = jnp.dot(normed_ref[...], w1_ref[...], preferred_element_type=F32)
    inner = (0.5 * hidden * (1.0 + lax.erf(hidden * math.sqrt(0.5)))).astype(BF16)
    result = jnp.dot(inner, w2_ref[...], preferred_element_type=F32)
    out_ref[...] = result.astype(out_ref.dtype)


def mlp(normed, w1, w2, kept_as):
    return pl.pallas_call(
        mlp_kernel,
        in_specs=[VM, VM, VM],
        out_specs=VM,
        out_shape=jax.ShapeDtypeStruct(normed.shape, kept_as),
        compiler_params=params(14),
        cost_estimate=cost(4 * normed.size * w1.shape[1], 4 * w1.size, 2 * normed.size),
        name="mlp",
    )(normed, w1, w2)


def kv_kernel(start, core_ref, live_ref, keys_ref, gain_ref, own_ref, send_ref):
    half = keys_ref.shape[1]
    block = own_ref.shape[1] // 2
    core = core_ref[0]
    slot = lax.broadcasted_iota(jnp.int32, (half, 1), 0) + core * (KI // 2) + start
    live = slot < live_ref[0] * TILE_TOK
    gain = gain_ref[...].reshape(1, -1)

    def write(ref, which):
        for head in range(block // HD):
            at = pl.ds(pl.multiple_of(which * block + head * HD, HD), HD)
            keys = rms_norm(keys_ref[0, :, at], gain)
            ref[:, head * HD : (head + 1) * HD] = keys.astype(BF16)
            values = keys_ref[1, :, at]
            ref[:, block + head * HD : block + (head + 1) * HD] = jnp.where(
                live, values, DEAD
            ).astype(BF16)

    write(send_ref, 1 - core)
    write(own_ref, core)


def finish_kv(start, core, live_tiles, key_value, gain):
    _, half, columns = key_value.shape
    return pl.pallas_call(
        functools.partial(kv_kernel, start),
        in_specs=[SM, SM, VM, VM],
        out_specs=[VM, VM],
        out_shape=[jax.ShapeDtypeStruct((half, columns), BF16)] * 2,
        compiler_params=params(8),
        cost_estimate=cost(10 * key_value.size, 6 * key_value.size),
        name="finish_kv",
    )(core, live_tiles, key_value, gain)


def query_kernel(line, mask_ref, seq_ref, text_ref, gain_ref, out_ref, flags_ref):
    kv_local, blocks, rows, _ = out_ref.shape
    group = rows // QB
    images = mask_ref.shape[0] // blocks
    lane = lax.broadcasted_iota(jnp.int32, (1, flags_ref.shape[1]), 1)
    for block in range(blocks):
        row = jnp.zeros_like(lane)
        seen = jnp.int32(0)
        for slot in range(images):
            image = seq_ref[0] ^ slot if line else slot
            flag = mask_ref[block * images + image]
            row = jnp.where(lane == slot, flag, row)
            seen = seen + flag
        flags_ref[block : block + 1, :] = row
        flags_ref[blocks + block : blocks + block + 1, :] = jnp.zeros_like(lane) + seen
    gain = gain_ref[...].reshape(1, -1)
    for head in range(kv_local):
        for block in range(blocks):
            for member in range(group):
                at = (head * group + member) * HD
                part = text_ref[block * QB : (block + 1) * QB, at : at + HD].astype(F32)
                out_ref[head, block, member * QB : (member + 1) * QB, :] = (
                    rms_norm(part, gain) * (1.0 / math.sqrt(HD))
                ).astype(BF16)


def norm_queries(line, mask, seq, text, gain, kv_local):
    rows, columns = text.shape
    group = columns // HD // kv_local
    blocks, images = mask.shape
    lanes = -(-images // 128) * 128
    return pl.pallas_call(
        functools.partial(query_kernel, line),
        in_specs=[SM, SM, VM, VM],
        out_specs=[VM, VM],
        out_shape=[
            jax.ShapeDtypeStruct((kv_local, rows // QB, group * QB, HD), BF16),
            jax.ShapeDtypeStruct((2 * blocks, lanes), jnp.int32),
        ],
        compiler_params=params(8),
        cost_estimate=cost(8 * rows * columns, 4 * rows * columns),
        name="norm_queries",
    )(mask.reshape(-1), seq, text, gain)


def cross_kernel(slots, images, first, last, flags_ref, q_ref, *refs):
    flat = sum(count for _, count in slots)
    kv_refs, refs = list(refs[:flat]), refs[flat:]
    refs = refs if first else refs[1:]
    kv_local, blocks, rows, _ = q_ref.shape
    group = rows // QB
    if last:
        out_hbm, acc, vals, out_ref, sems = refs
    else:
        acc, vals = refs

    def wanted(block, image):
        if isinstance(image, int):
            return flags_ref[block : block + 1, image : image + 1][0, 0] > 0
        row = flags_ref[block : block + 1, :]
        lane = lax.broadcasted_iota(jnp.int32, row.shape, 1)
        return jnp.max(jnp.where(lane == image, row, 0)) > 0

    def attend(block, head, member, chunks):
        at = slice(member * QB, (member + 1) * QB)
        keys = [kv[:, head * HD : (head + 1) * HD] for kv in chunks]
        keys = keys[0] if len(keys) == 1 else jnp.concatenate(keys, axis=0)
        sims = lax.dot_general(q_ref[head, block, at, :], keys, NT, preferred_element_type=F32)
        return jnp.dot(jnp.exp(sims).astype(BF16), vals[head], preferred_element_type=F32)

    def one_image(image, chunks, fresh):
        some = functools.reduce(jnp.logical_or, [wanted(block, image) for block in range(blocks)])

        @pl.when(some)
        def _():
            for head in range(kv_local):
                at = 0
                for kv in chunks:
                    values = kv[:, (kv_local + head) * HD : (kv_local + head + 1) * HD]
                    live = values < DEAD * 0.5
                    span = slice(at, at + values.shape[0])
                    vals[head, span, :HD] = jnp.where(live, values, jnp.zeros_like(values))
                    vals[head, span, HD:] = jnp.where(live, 1.0, 0.0).astype(BF16)
                    at += values.shape[0]

        for block in range(blocks):

            @pl.when(wanted(block, image))
            def _(block=block):
                for head in range(kv_local):
                    for member in range(group):
                        at = slice(member * QB, (member + 1) * QB)
                        more = attend(block, head, member, chunks)
                        acc[head, block, at, :] = more if fresh else acc[head, block, at, :] + more

            if fresh:

                @pl.when(jnp.logical_not(wanted(block, image)))
                def _(block=block):
                    acc[:, block] = jnp.zeros((kv_local, rows, 2 * HD), F32)

    if slots[0][0] is None:
        acc[...] = jnp.zeros_like(acc)

        @pl.loop(0, images)
        def _(image):
            one_image(image, [kv_refs[0].at[image]], False)
    else:
        for number, (bits, count) in enumerate(slots):
            one_image(bits, [kv_refs.pop(0) for _ in range(count)], first and number == 0)

    if not last:
        return
    span = group * HD
    copies = {}
    for block in range(blocks):
        seen = flags_ref[blocks + block : blocks + block + 1, :1][0, 0]
        for head in range(kv_local):
            rows_at = slice(block * QB, (block + 1) * QB)
            columns = slice(head * span, (head + 1) * span)

            @pl.when(seen > 0)
            def _(head=head, block=block, rows_at=rows_at):
                for member in range(group):
                    at = slice(member * QB, (member + 1) * QB)
                    column = (head * group + member) * HD
                    out_ref[rows_at, column : column + HD] = (
                        acc[head, block, at, :HD] / acc[head, block, at, HD:]
                    ).astype(BF16)

            @pl.when(seen == 0)
            def _(rows_at=rows_at, columns=columns):
                out_ref[rows_at, columns] = jnp.zeros((QB, span), BF16)

            copies[block, head] = pltpu.make_async_copy(
                out_ref.at[rows_at, columns], out_hbm.at[rows_at, columns], sems.at[block, head]
            )
            copies[block, head].start()
    for copy in copies.values():
        copy.wait()


def cross(images, flags, queries, slots, acc=None, last=True):
    kv_local, blocks, rows, _ = queries.shape
    flat = [chunk for _, chunks in slots for chunk in chunks]
    keys = sum(chunk.shape[-2] for chunk in slots[0][1])
    out = jax.ShapeDtypeStruct((blocks * QB, kv_local * (rows // QB) * HD), BF16)
    work = blocks * rows * sum(kv.size for kv in flat) // (2 * HD)
    sums = (kv_local, blocks, rows, 2 * HD)
    given = [] if acc is None else [acc]
    scratch = [pltpu.VMEM((kv_local, keys, 2 * HD), BF16)]
    if last:
        scratch += [pltpu.VMEM(out.shape, BF16), pltpu.SemaphoreType.DMA((blocks, kv_local))]
    result = pl.pallas_call(
        functools.partial(
            cross_kernel,
            [(bits, len(chunks)) for bits, chunks in slots],
            images,
            acc is None,
            last,
        ),
        in_specs=[VM, VM] + [VM] * len(flat + given),
        out_specs=[HB, VM] if last else [VM],
        out_shape=[out] * last + [jax.ShapeDtypeStruct(sums, F32)],
        scratch_shapes=scratch,
        input_output_aliases={2 + len(flat): int(last)} if given else {},
        compiler_params=params(14),
        cost_estimate=cost(4 * work * HD, 4 * queries.size, work),
        name="cross",
    )(flags, queries, *flat, *given)
    return result[0]


def swap_line(bits, value):
    return lax.ppermute(value, "seq", [(s, s ^ bits) for s in range(8)])


def tie(values, *after):
    return lax.optimization_barrier((tuple(values), after))[0]


def gather_line(blocks, attend):
    images = []
    for block in blocks:
        images.append({0: block, 4: swap_line(4, block), 2: swap_line(2, block)})
    crossed = []

    def swap_x(value):
        if len(crossed) > 1:
            value = tie((value,), crossed[-2])[0]
        crossed.append(swap_line(1, value))
        return crossed[-1]

    def slots(*several):
        return [(bits, [got[bits] for got in images]) for bits in several]

    for got in images:
        got[1] = swap_x(got[0])
    acc = None
    for got, several in zip(images, EARLY):
        acc = attend(slots(*several), acc, False)
        far, near, acc = tie((got[4], got[2], acc))
        got[3] = swap_x(near)
        got[6] = swap_line(2, far)
        got[5] = swap_x(far)
    for number, got in enumerate(images):
        if number == len(images) - 1 and number > 0:
            got[7] = swap_line(2, got[5])
        else:
            got[7] = swap_x(got[6])
    for several in LATE:
        acc = attend(slots(*several), acc, several == LATE[-1])
    return acc


def per_device(
    vis_in,
    live_tiles,
    ln1_gain,
    w_qkv,
    w_out,
    ln2_gain,
    w_fc1,
    w_fc2,
    w_kv,
    k_gain,
    q_gain,
    text_queries,
    block_mask,
):
    head_count = lax.axis_size("head")
    head_index = lax.axis_index("head")
    core = head_index % 2
    core_arg = core.astype(jnp.int32).reshape(1)
    kv_local = KVH // head_count
    swap_core = functools.partial(
        lax.ppermute, axis_name="head", perm=[(i, i ^ 1) for i in range(head_count)]
    )

    def swap_chip(value, bit):
        return lax.ppermute(value, "head", [(i, i ^ bit) for i in range(head_count)])

    def sum_chips(value):
        bit = 2
        other = swap_chip(value, bit)
        while 2 * bit < head_count:
            bit *= 2
            value = (value.astype(F32) + other.astype(F32)).astype(BF16)
            other = swap_chip(value, bit)
        return value, other

    x = vis_in.reshape(vis_in.shape[0] * vis_in.shape[1], vis_in.shape[2])
    rows, width = x.shape
    half = rows // 2
    line = lax.axis_size("seq") == 8
    cuts = [0, half * FIRST // 128, half] if line else [0, half]
    chunks = [slice(at, end) for at, end in zip(cuts, cuts[1:])]
    chip_columns = 2 * kv_local * HD

    seq = lax.axis_index("seq").astype(jnp.int32).reshape(1)
    images = block_mask.shape[1]
    queries, flags = norm_queries(line, block_mask, seq, text_queries, q_gain, kv_local)
    send, kept, own_x = encode(
        core_arg, live_tiles, x, ln1_gain, jnp.swapaxes(w_qkv, 1, 2), w_out
    )
    received = swap_core(send)
    chip_arg = (head_index // 2).astype(jnp.int32).reshape(1)
    first = (kept + received.astype(F32)).astype(BF16)
    w1, w2, w_chip = fetch(chip_arg, w_fc1, w_fc2, w_kv, chip_columns, first)
    first, second = sum_chips(first)
    resid, normed = mid(own_x, first, second, ln2_gain, w_chip, queries)
    other = swap_core(normed)
    keep = mlp(normed, w1, w2, F32)
    received = swap_core(mlp(other, w1, w2, BF16))
    sums = [(keep[at] + received[at].astype(F32)).astype(BF16) for at in chunks]
    sums = [sum_chips(value) for value in sums]
    blocks = []
    for at, (first, second) in zip(chunks, sums):
        second = tie((second,), blocks[-1] if blocks else sums[-1][0])[0]
        vision = (resid[at] + (first.astype(F32) + second.astype(F32))).astype(BF16)
        key_value = jnp.einsum("rc,cjd->jrd", vision, w_chip, preferred_element_type=F32)
        own, send = finish_kv(at.start, core_arg, live_tiles, key_value, k_gain)
        blocks.append(jnp.concatenate([own, swap_core(send)], axis=0))

    if not line:
        stacked = lax.all_gather(jnp.concatenate(blocks, axis=0), "seq", axis=0)
        return cross(images, flags, queries, [(None, [stacked])])
    return gather_line(blocks, functools.partial(cross, images, flags, queries))


def solution(mesh):
    placed = (
        P("seq", None, None),
        P("seq"),
        P(),
        P(None, None, "head"),
        P("head", None),
        P(),
        P(None, "head"),
        P("head", None),
        P(),
        P(),
        P(),
        P("seq", "head"),
        P("seq", None),
    )
    return jax.shard_map(
        per_device, mesh=mesh, in_specs=placed, out_specs=P("seq", "head"), check_vma=False
    )
```

```python
import functools
import math

import jax
import jax.numpy as jnp
from jax import lax
from jax.experimental import pallas as pl
from jax.experimental.pallas import tpu as pltpu
from jax.sharding import PartitionSpec as P

KVH = 8
HD = 128
TILE_TOK = 64
QB = 128
VHD = 80
KI = 256
DEAD = 1e30
FIRST = 64
EARLY = [[0], [2, 1]]
LATE = [[4, 3], [5, 6], [7]]
F32 = jnp.float32
BF16 = jnp.bfloat16

NT = (((1,), (1,)), ((), ()))
VM = pl.BlockSpec(memory_space=pltpu.VMEM)
SM = pl.BlockSpec(memory_space=pltpu.SMEM)
HB = pl.BlockSpec(memory_space=pltpu.HBM)
AN = pl.BlockSpec(memory_space=pl.ANY)


def params(mib):
    return pltpu.CompilerParams(vmem_limit_bytes=mib * 1024 * 1024)


def in_hbm(value):
    return pltpu.with_memory_space_constraint(value, pltpu.HBM)


def cost(flops, size, transcendentals=0):
    return pl.CostEstimate(flops=flops, bytes_accessed=size, transcendentals=transcendentals)


def layer_norm(values, gain):
    center = values - jnp.mean(values, axis=-1, keepdims=True)
    spread = jnp.mean(center * center, axis=-1, keepdims=True)
    return center * (1.0 / jnp.sqrt(spread + 1e-05)) * gain


def rms_norm(values, gain):
    square = jnp.mean(values * values, axis=-1, keepdims=True)
    return values * (1.0 / jnp.sqrt(square + 1e-05)) * gain


def encode_kernel(
    core_ref,
    live_ref,
    gain_hbm,
    x_hbm,
    wqkv_hbm,
    wout_hbm,
    send_ref,
    keep_ref,
    own_ref,
    gain_ref,
    x_ref,
    wqkv_ref,
    wout_ref,
    mixed_ref,
    sems,
):
    loads = [pltpu.make_async_copy(x_hbm, x_ref, sems.at[0])]
    loads += [
        pltpu.make_async_copy(wqkv_hbm.at[j], wqkv_ref.at[j], sems.at[1 + j]) for j in range(3)
    ]
    loads.append(pltpu.make_async_copy(wout_hbm, wout_ref, sems.at[4]))
    loads.append(pltpu.make_async_copy(gain_hbm, gain_ref, sems.at[5]))
    for load in loads:
        load.start()
    rows, width = mixed_ref.shape
    half = rows // 2
    core = core_ref[0]
    own_rows = pl.ds(pl.multiple_of(core * half, half), half)
    other_rows = pl.ds(pl.multiple_of((1 - core) * half, half), half)

    loads[0].wait()
    loads[5].wait()
    own_ref[...] = x_ref[own_rows, :]
    normed = layer_norm(x_ref[...].astype(F32), gain_ref[...].reshape(1, -1)).astype(BF16)
    for load in loads[1:4]:
        load.wait()
    weights = wqkv_ref[...].reshape(3 * width, x_ref.shape[1])
    qkv = lax.dot_general(normed, weights, NT, preferred_element_type=F32).astype(BF16)
    q, k, v = [qkv[:, j * width : (j + 1) * width] for j in range(3)]
    lane = lax.broadcasted_iota(jnp.int32, (1, width), 1)
    slot = lax.broadcasted_iota(jnp.int32, (1, rows), 1)
    live = jnp.where(slot < live_ref[0] * TILE_TOK, 1.0, 0.0).astype(F32)
    zero = jnp.zeros_like(q)
    mixed = jnp.zeros((rows, width), F32)
    for head in range(width // VHD):
        own = (lane >= head * VHD) & (lane < (head + 1) * VHD)
        scores = lax.dot_general(jnp.where(own, q, zero), k, NT, preferred_element_type=F32)
        expo = jnp.exp(scores * (1.0 / math.sqrt(VHD))) * live
        probs = (expo * (1.0 / jnp.sum(expo, axis=-1, keepdims=True))).astype(BF16)
        mixed = mixed + jnp.dot(probs, jnp.where(own, v, zero), preferred_element_type=F32)
    mixed_ref[...] = mixed.astype(BF16)
    loads[4].wait()
    send_ref[...] = jnp.dot(
        mixed_ref[other_rows, :], wout_ref[...], preferred_element_type=F32
    ).astype(BF16)
    keep_ref[...] = jnp.dot(mixed_ref[own_rows, :], wout_ref[...], preferred_element_type=F32)


def encode(core, live_tiles, x, gain, w_qkv_t, w_out):
    rows, width = x.shape
    own = w_out.shape[0]
    return pl.pallas_call(
        encode_kernel,
        in_specs=[SM, SM, HB, HB, HB, HB],
        out_specs=[VM, VM, VM],
        out_shape=[
            jax.ShapeDtypeStruct((rows // 2, width), BF16),
            jax.ShapeDtypeStruct((rows // 2, width), F32),
            jax.ShapeDtypeStruct((rows // 2, width), BF16),
        ],
        scratch_shapes=[
            pltpu.VMEM(gain.shape, F32),
            pltpu.VMEM(x.shape, BF16),
            pltpu.VMEM(w_qkv_t.shape, BF16),
            pltpu.VMEM(w_out.shape, BF16),
            pltpu.VMEM((rows, own), BF16),
            pltpu.SemaphoreType.DMA((6,)),
        ],
        compiler_params=params(12),
        cost_estimate=cost(2 * rows * width * 4 * own, 8 * width * own, rows * rows * own // VHD),
        name="encode",
    )(core, live_tiles, in_hbm(gain), in_hbm(x), in_hbm(w_qkv_t), in_hbm(w_out))


def mid_kernel(x_ref, first_ref, second_ref, gain_ref, _, __, resid_ref, normed_ref):
    resid = x_ref[...].astype(F32) + (first_ref[...].astype(F32) + second_ref[...].astype(F32))
    resid_ref[...] = resid
    normed_ref[...] = layer_norm(resid, gain_ref[...].reshape(1, -1)).astype(BF16)


def mid(x, first, second, gain, *after):
    half, width = first.shape
    return pl.pallas_call(
        mid_kernel,
        in_specs=[VM, VM, VM, VM, AN, AN],
        out_specs=[VM, VM],
        out_shape=[
            jax.ShapeDtypeStruct((half, width), F32),
            jax.ShapeDtypeStruct((half, width), BF16),
        ],
        compiler_params=params(8),
        cost_estimate=cost(10 * half * width, 14 * half * width),
        name="mid",
    )(x, first, second, gain, *after)


def fetch_kernel(chip_ref, w1_hbm, w2_hbm, wkv_hbm, _, w1_ref, w2_ref, wkv_ref, sems):
    columns = wkv_ref.shape[2]
    mine = pl.ds(pl.multiple_of(chip_ref[0] * columns, HD), columns)
    loads = [
        pltpu.make_async_copy(w1_hbm, w1_ref, sems.at[0]),
        pltpu.make_async_copy(w2_hbm, w2_ref, sems.at[1]),
        pltpu.make_async_copy(wkv_hbm.at[:, :, mine], wkv_ref, sems.at[2]),
    ]
    for load in loads:
        load.start()
    for load in loads:
        load.wait()


def fetch(chip, w1, w2, w_kv, columns, after):
    shapes = [w1.shape, w2.shape, (w_kv.shape[0], w_kv.shape[1], columns)]
    return pl.pallas_call(
        fetch_kernel,
        in_specs=[SM, HB, HB, HB, AN],
        out_specs=[VM, VM, VM],
        out_shape=[jax.ShapeDtypeStruct(shape, BF16) for shape in shapes],
        scratch_shapes=[pltpu.SemaphoreType.DMA((3,))],
        compiler_params=params(16),
        cost_estimate=cost(0, 20 * w1.size),
        name="fetch",
    )(chip, in_hbm(w1), in_hbm(w2), in_hbm(w_kv), after)


def mlp_kernel(normed_ref, w1_ref, w2_ref, out_ref):
    hidden = jnp.dot(normed_ref[...], w1_ref[...], preferred_element_type=F32)
    inner = (0.5 * hidden * (1.0 + lax.erf(hidden * math.sqrt(0.5)))).astype(BF16)
    result = jnp.dot(inner, w2_ref[...], preferred_element_type=F32)
    out_ref[...] = result.astype(out_ref.dtype)


def mlp(normed, w1, w2, kept_as):
    return pl.pallas_call(
        mlp_kernel,
        in_specs=[VM, VM, VM],
        out_specs=VM,
        out_shape=jax.ShapeDtypeStruct(normed.shape, kept_as),
        compiler_params=params(14),
        cost_estimate=cost(4 * normed.size * w1.shape[1], 4 * w1.size, 2 * normed.size),
        name="mlp",
    )(normed, w1, w2)


def kv_kernel(start, core_ref, live_ref, keys_ref, gain_ref, own_ref, send_ref):
    half = keys_ref.shape[1]
    block = own_ref.shape[1] // 2
    core = core_ref[0]
    slot = lax.broadcasted_iota(jnp.int32, (half, 1), 0) + core * (KI // 2) + start
    live = slot < live_ref[0] * TILE_TOK
    gain = gain_ref[...].reshape(1, -1)

    def write(ref, which):
        for head in range(block // HD):
            at = pl.ds(pl.multiple_of(which * block + head * HD, HD), HD)
            keys = rms_norm(keys_ref[0, :, at], gain)
            ref[:, head * HD : (head + 1) * HD] = keys.astype(BF16)
            values = keys_ref[1, :, at]
            ref[:, block + head * HD : block + (head + 1) * HD] = jnp.where(
                live, values, DEAD
            ).astype(BF16)

    write(send_ref, 1 - core)
    write(own_ref, core)


def finish_kv(start, core, live_tiles, key_value, gain):
    _, half, columns = key_value.shape
    return pl.pallas_call(
        functools.partial(kv_kernel, start),
        in_specs=[SM, SM, VM, VM],
        out_specs=[VM, VM],
        out_shape=[jax.ShapeDtypeStruct((half, columns), BF16)] * 2,
        compiler_params=params(8),
        cost_estimate=cost(10 * key_value.size, 6 * key_value.size),
        name="finish_kv",
    )(core, live_tiles, key_value, gain)


def query_kernel(line, mask_ref, seq_ref, core_ref, text_ref, gain_ref, out_ref, flags_ref):
    kv_local, blocks, rows, _ = out_ref.shape
    group = rows // QB
    images = mask_ref.shape[0] // blocks
    lane = lax.broadcasted_iota(jnp.int32, (1, flags_ref.shape[1]), 1)
    for block in range(blocks):
        row = jnp.zeros_like(lane)
        seen = jnp.int32(0)
        for slot in range(images):
            image = slot
            if line:
                turned = (slot & 4) | (slot & 1) << 1 | (slot & 2) >> 1
                image = seq_ref[0] ^ jnp.where(core_ref[0] == 0, slot, turned)
            flag = mask_ref[block * images + image]
            row = jnp.where(lane == slot, flag, row)
            seen = seen + flag
        flags_ref[block : block + 1, :] = row
        flags_ref[blocks + block : blocks + block + 1, :] = jnp.zeros_like(lane) + seen
    gain = gain_ref[...].reshape(1, -1)
    for head in range(kv_local):
        for block in range(blocks):
            for member in range(group):
                at = (head * group + member) * HD
                part = text_ref[block * QB : (block + 1) * QB, at : at + HD].astype(F32)
                out_ref[head, block, member * QB : (member + 1) * QB, :] = (
                    rms_norm(part, gain) * (1.0 / math.sqrt(HD))
                ).astype(BF16)


def norm_queries(line, mask, seq, core, text, gain, kv_local):
    rows, columns = text.shape
    group = columns // HD // kv_local
    blocks, images = mask.shape
    lanes = -(-images // 128) * 128
    return pl.pallas_call(
        functools.partial(query_kernel, line),
        in_specs=[SM, SM, SM, VM, VM],
        out_specs=[VM, VM],
        out_shape=[
            jax.ShapeDtypeStruct((kv_local, rows // QB, group * QB, HD), BF16),
            jax.ShapeDtypeStruct((2 * blocks, lanes), jnp.int32),
        ],
        compiler_params=params(8),
        cost_estimate=cost(8 * rows * columns, 4 * rows * columns),
        name="norm_queries",
    )(mask.reshape(-1), seq, core, text, gain)


def cross_kernel(slots, images, first, last, flags_ref, q_ref, *refs):
    flat = sum(count for _, count in slots)
    kv_refs, refs = list(refs[:flat]), refs[flat:]
    refs = refs if first else refs[1:]
    kv_local, blocks, rows, _ = q_ref.shape
    group = rows // QB
    if last:
        out_hbm, acc, vals, out_ref, sems = refs
    else:
        acc, vals = refs

    def wanted(block, image):
        if isinstance(image, int):
            return flags_ref[block : block + 1, image : image + 1][0, 0] > 0
        row = flags_ref[block : block + 1, :]
        lane = lax.broadcasted_iota(jnp.int32, row.shape, 1)
        return jnp.max(jnp.where(lane == image, row, 0)) > 0

    def attend(block, head, member, chunks):
        at = slice(member * QB, (member + 1) * QB)
        keys = [kv[:, head * HD : (head + 1) * HD] for kv in chunks]
        keys = keys[0] if len(keys) == 1 else jnp.concatenate(keys, axis=0)
        sims = lax.dot_general(q_ref[head, block, at, :], keys, NT, preferred_element_type=F32)
        return jnp.dot(jnp.exp(sims).astype(BF16), vals[head], preferred_element_type=F32)

    def one_image(image, chunks, fresh):
        some = functools.reduce(jnp.logical_or, [wanted(block, image) for block in range(blocks)])

        @pl.when(some)
        def _():
            for head in range(kv_local):
                at = 0
                for kv in chunks:
                    values = kv[:, (kv_local + head) * HD : (kv_local + head + 1) * HD]
                    live = values < DEAD * 0.5
                    span = slice(at, at + values.shape[0])
                    vals[head, span, :HD] = jnp.where(live, values, jnp.zeros_like(values))
                    vals[head, span, HD:] = jnp.where(live, 1.0, 0.0).astype(BF16)
                    at += values.shape[0]

        for block in range(blocks):

            @pl.when(wanted(block, image))
            def _(block=block):
                for head in range(kv_local):
                    for member in range(group):
                        at = slice(member * QB, (member + 1) * QB)
                        more = attend(block, head, member, chunks)
                        acc[head, block, at, :] = more if fresh else acc[head, block, at, :] + more

            if fresh:

                @pl.when(jnp.logical_not(wanted(block, image)))
                def _(block=block):
                    acc[:, block] = jnp.zeros((kv_local, rows, 2 * HD), F32)

    if slots[0][0] is None:
        acc[...] = jnp.zeros_like(acc)

        @pl.loop(0, images)
        def _(image):
            one_image(image, [kv_refs[0].at[image]], False)
    else:
        for number, (bits, count) in enumerate(slots):
            one_image(bits, [kv_refs.pop(0) for _ in range(count)], first and number == 0)

    if not last:
        return
    span = group * HD
    copies = {}
    for block in range(blocks):
        seen = flags_ref[blocks + block : blocks + block + 1, :1][0, 0]
        for head in range(kv_local):
            rows_at = slice(block * QB, (block + 1) * QB)
            columns = slice(head * span, (head + 1) * span)

            @pl.when(seen > 0)
            def _(head=head, block=block, rows_at=rows_at):
                for member in range(group):
                    at = slice(member * QB, (member + 1) * QB)
                    column = (head * group + member) * HD
                    out_ref[rows_at, column : column + HD] = (
                        acc[head, block, at, :HD] / acc[head, block, at, HD:]
                    ).astype(BF16)

            @pl.when(seen == 0)
            def _(rows_at=rows_at, columns=columns):
                out_ref[rows_at, columns] = jnp.zeros((QB, span), BF16)

            copies[block, head] = pltpu.make_async_copy(
                out_ref.at[rows_at, columns], out_hbm.at[rows_at, columns], sems.at[block, head]
            )
            copies[block, head].start()
    for copy in copies.values():
        copy.wait()


def cross(images, flags, queries, slots, acc=None, last=True):
    kv_local, blocks, rows, _ = queries.shape
    flat = [chunk for _, chunks in slots for chunk in chunks]
    keys = sum(chunk.shape[-2] for chunk in slots[0][1])
    out = jax.ShapeDtypeStruct((blocks * QB, kv_local * (rows // QB) * HD), BF16)
    work = blocks * rows * sum(kv.size for kv in flat) // (2 * HD)
    sums = (kv_local, blocks, rows, 2 * HD)
    given = [] if acc is None else [acc]
    scratch = [pltpu.VMEM((kv_local, keys, 2 * HD), BF16)]
    if last:
        scratch += [pltpu.VMEM(out.shape, BF16), pltpu.SemaphoreType.DMA((blocks, kv_local))]
    result = pl.pallas_call(
        functools.partial(
            cross_kernel,
            [(bits, len(chunks)) for bits, chunks in slots],
            images,
            acc is None,
            last,
        ),
        in_specs=[VM, VM] + [VM] * len(flat + given),
        out_specs=[HB, VM] if last else [VM],
        out_shape=[out] * last + [jax.ShapeDtypeStruct(sums, F32)],
        scratch_shapes=scratch,
        input_output_aliases={2 + len(flat): int(last)} if given else {},
        compiler_params=params(14),
        cost_estimate=cost(4 * work * HD, 4 * queries.size, work),
        name="cross",
    )(flags, queries, *flat, *given)
    return result[0]


def swap_line(value, even, odd):
    heads = lax.axis_size("head")
    pairs = []
    for seq in range(lax.axis_size("seq")):
        for head in range(heads):
            other = seq ^ (odd if head % 2 else even)
            pairs.append((seq * heads + head, other * heads + head))
    return lax.ppermute(value, ("seq", "head"), pairs)


def tie(values, *after):
    return lax.optimization_barrier((tuple(values), after))[0]


def gather_line(blocks, attend):
    crossed = []

    def one(value):
        if len(crossed) > 1:
            value = tie((value,), crossed[-2])[0]
        crossed.append(swap_line(value, 1, 2))
        return crossed[-1]

    def two(value):
        return swap_line(value, 2, 1)

    def slots(*several):
        return [(bits, [got[bits] for got in images]) for bits in several]

    images = [{0: block, 4: swap_line(block, 4, 4)} for block in blocks]
    for got in images:
        got[1] = one(got[0])
    for got in images:
        got[2] = two(got[0])
    for got in images:
        got[6] = two(got[4])
        got[5] = one(got[4])
        got[3] = one(got[2])
    images[0][7] = one(images[0][6])
    images[1][7] = two(images[1][5])
    acc = None
    for several in ((0,), (2, 1), (4, 3), (5, 6), (7,)):
        acc = attend(slots(*several), acc, several == (7,))
    return acc


def per_device(
    vis_in,
    live_tiles,
    ln1_gain,
    w_qkv,
    w_out,
    ln2_gain,
    w_fc1,
    w_fc2,
    w_kv,
    k_gain,
    q_gain,
    text_queries,
    block_mask,
):
    head_count = lax.axis_size("head")
    head_index = lax.axis_index("head")
    core = head_index % 2
    core_arg = core.astype(jnp.int32).reshape(1)
    kv_local = KVH // head_count
    swap_core = functools.partial(
        lax.ppermute, axis_name="head", perm=[(i, i ^ 1) for i in range(head_count)]
    )

    def swap_chip(value, bit):
        return lax.ppermute(value, "head", [(i, i ^ bit) for i in range(head_count)])

    def sum_chips(value):
        bit = 2
        other = swap_chip(value, bit)
        while 2 * bit < head_count:
            bit *= 2
            value = (value.astype(F32) + other.astype(F32)).astype(BF16)
            other = swap_chip(value, bit)
        return value, other

    x = vis_in.reshape(vis_in.shape[0] * vis_in.shape[1], vis_in.shape[2])
    rows, width = x.shape
    half = rows // 2
    line = lax.axis_size("seq") == 8
    cuts = [0, half * FIRST // 128, half] if line else [0, half]
    chunks = [slice(at, end) for at, end in zip(cuts, cuts[1:])]
    chip_columns = 2 * kv_local * HD

    seq = lax.axis_index("seq").astype(jnp.int32).reshape(1)
    images = block_mask.shape[1]
    queries, flags = norm_queries(line, block_mask, seq, core_arg, text_queries, q_gain, kv_local)
    send, kept, own_x = encode(
        core_arg, live_tiles, x, ln1_gain, jnp.swapaxes(w_qkv, 1, 2), w_out
    )
    received = swap_core(send)
    chip_arg = (head_index // 2).astype(jnp.int32).reshape(1)
    first = (kept + received.astype(F32)).astype(BF16)
    w1, w2, w_chip = fetch(chip_arg, w_fc1, w_fc2, w_kv, chip_columns, first)
    first, second = sum_chips(first)
    resid, normed = mid(own_x, first, second, ln2_gain, w_chip, queries)
    other = swap_core(normed)
    keep = mlp(normed, w1, w2, F32)
    received = swap_core(mlp(other, w1, w2, BF16))
    sums = [(keep[at] + received[at].astype(F32)).astype(BF16) for at in chunks]
    sums = [sum_chips(value) for value in sums]
    blocks = []
    for at, (first, second) in zip(chunks, sums):
        second = tie((second,), blocks[-1] if blocks else sums[-1][0])[0]
        vision = (resid[at] + (first.astype(F32) + second.astype(F32))).astype(BF16)
        key_value = jnp.einsum("rc,cjd->jrd", vision, w_chip, preferred_element_type=F32)
        own, send = finish_kv(at.start, core_arg, live_tiles, key_value, k_gain)
        blocks.append(jnp.concatenate([own, swap_core(send)], axis=0))

    if not line:
        stacked = lax.all_gather(jnp.concatenate(blocks, axis=0), "seq", axis=0)
        return cross(images, flags, queries, [(None, [stacked])])
    return gather_line(blocks, functools.partial(cross, images, flags, queries))


def solution(mesh):
    placed = (
        P("seq", None, None),
        P("seq"),
        P(),
        P(None, None, "head"),
        P("head", None),
        P(),
        P(None, "head"),
        P("head", None),
        P(),
        P(),
        P(),
        P("seq", "head"),
        P("seq", None),
    )
    return jax.shard_map(
        per_device, mesh=mesh, in_specs=placed, out_specs=P("seq", "head"), check_vma=False
    )
```

```python
import functools
import math

import jax
import jax.numpy as jnp
from jax import lax
from jax.experimental import pallas as pl
from jax.experimental.pallas import tpu as pltpu
from jax.sharding import PartitionSpec as P

KVH = 8
HD = 128
TILE_TOK = 64
QB = 128
VHD = 80
KI = 256
DEAD = 1e30
FIRST = 64
EARLY = [[0], [2, 1]]
LATE = [[4, 3], [5, 6], [7]]
F32 = jnp.float32
BF16 = jnp.bfloat16

NT = (((1,), (1,)), ((), ()))
VM = pl.BlockSpec(memory_space=pltpu.VMEM)
SM = pl.BlockSpec(memory_space=pltpu.SMEM)
HB = pl.BlockSpec(memory_space=pltpu.HBM)
AN = pl.BlockSpec(memory_space=pl.ANY)


def params(mib):
    return pltpu.CompilerParams(vmem_limit_bytes=mib * 1024 * 1024)


def in_hbm(value):
    return pltpu.with_memory_space_constraint(value, pltpu.HBM)


def cost(flops, size, transcendentals=0):
    return pl.CostEstimate(flops=flops, bytes_accessed=size, transcendentals=transcendentals)


def layer_norm(values, gain):
    center = values - jnp.mean(values, axis=-1, keepdims=True)
    spread = jnp.mean(center * center, axis=-1, keepdims=True)
    return center * (1.0 / jnp.sqrt(spread + 1e-05)) * gain


def rms_norm(values, gain):
    square = jnp.mean(values * values, axis=-1, keepdims=True)
    return values * (1.0 / jnp.sqrt(square + 1e-05)) * gain


def encode_kernel(
    core_ref,
    live_ref,
    gain_hbm,
    x_hbm,
    wqkv_hbm,
    wout_hbm,
    send_ref,
    keep_ref,
    own_ref,
    gain_ref,
    x_ref,
    wqkv_ref,
    wout_ref,
    mixed_ref,
    sems,
):
    loads = [pltpu.make_async_copy(x_hbm, x_ref, sems.at[0])]
    loads += [
        pltpu.make_async_copy(wqkv_hbm.at[j], wqkv_ref.at[j], sems.at[1 + j]) for j in range(3)
    ]
    loads.append(pltpu.make_async_copy(wout_hbm, wout_ref, sems.at[4]))
    loads.append(pltpu.make_async_copy(gain_hbm, gain_ref, sems.at[5]))
    for load in loads:
        load.start()
    rows, width = mixed_ref.shape
    half = rows // 2
    core = core_ref[0]
    own_rows = pl.ds(pl.multiple_of(core * half, half), half)
    other_rows = pl.ds(pl.multiple_of((1 - core) * half, half), half)

    loads[0].wait()
    loads[5].wait()
    own_ref[...] = x_ref[own_rows, :]
    normed = layer_norm(x_ref[...].astype(F32), gain_ref[...].reshape(1, -1)).astype(BF16)
    for load in loads[1:4]:
        load.wait()
    weights = wqkv_ref[...].reshape(3 * width, x_ref.shape[1])
    qkv = lax.dot_general(normed, weights, NT, preferred_element_type=F32).astype(BF16)
    q, k, v = [qkv[:, j * width : (j + 1) * width] for j in range(3)]
    lane = lax.broadcasted_iota(jnp.int32, (1, width), 1)
    slot = lax.broadcasted_iota(jnp.int32, (1, rows), 1)
    live = jnp.where(slot < live_ref[0] * TILE_TOK, 1.0, 0.0).astype(F32)
    zero = jnp.zeros_like(q)
    mixed = jnp.zeros((rows, width), F32)
    for head in range(width // VHD):
        own = (lane >= head * VHD) & (lane < (head + 1) * VHD)
        scores = lax.dot_general(jnp.where(own, q, zero), k, NT, preferred_element_type=F32)
        expo = jnp.exp(scores * (1.0 / math.sqrt(VHD))) * live
        probs = (expo * (1.0 / jnp.sum(expo, axis=-1, keepdims=True))).astype(BF16)
        mixed = mixed + jnp.dot(probs, jnp.where(own, v, zero), preferred_element_type=F32)
    mixed_ref[...] = mixed.astype(BF16)
    loads[4].wait()
    send_ref[...] = jnp.dot(
        mixed_ref[other_rows, :], wout_ref[...], preferred_element_type=F32
    ).astype(BF16)
    keep_ref[...] = jnp.dot(mixed_ref[own_rows, :], wout_ref[...], preferred_element_type=F32)


def encode(core, live_tiles, x, gain, w_qkv_t, w_out):
    rows, width = x.shape
    own = w_out.shape[0]
    return pl.pallas_call(
        encode_kernel,
        in_specs=[SM, SM, HB, HB, HB, HB],
        out_specs=[VM, VM, VM],
        out_shape=[
            jax.ShapeDtypeStruct((rows // 2, width), BF16),
            jax.ShapeDtypeStruct((rows // 2, width), F32),
            jax.ShapeDtypeStruct((rows // 2, width), BF16),
        ],
        scratch_shapes=[
            pltpu.VMEM(gain.shape, F32),
            pltpu.VMEM(x.shape, BF16),
            pltpu.VMEM(w_qkv_t.shape, BF16),
            pltpu.VMEM(w_out.shape, BF16),
            pltpu.VMEM((rows, own), BF16),
            pltpu.SemaphoreType.DMA((6,)),
        ],
        compiler_params=params(12),
        cost_estimate=cost(2 * rows * width * 4 * own, 8 * width * own, rows * rows * own // VHD),
        name="encode",
    )(core, live_tiles, in_hbm(gain), in_hbm(x), in_hbm(w_qkv_t), in_hbm(w_out))


def mid_kernel(x_ref, first_ref, second_ref, gain_ref, _, __, resid_ref, normed_ref):
    resid = x_ref[...].astype(F32) + (first_ref[...].astype(F32) + second_ref[...].astype(F32))
    resid_ref[...] = resid
    normed_ref[...] = layer_norm(resid, gain_ref[...].reshape(1, -1)).astype(BF16)


def mid(x, first, second, gain, *after):
    half, width = first.shape
    return pl.pallas_call(
        mid_kernel,
        in_specs=[VM, VM, VM, VM, AN, AN],
        out_specs=[VM, VM],
        out_shape=[
            jax.ShapeDtypeStruct((half, width), F32),
            jax.ShapeDtypeStruct((half, width), BF16),
        ],
        compiler_params=params(8),
        cost_estimate=cost(10 * half * width, 14 * half * width),
        name="mid",
    )(x, first, second, gain, *after)


def fetch_kernel(chip_ref, w1_hbm, w2_hbm, wkv_hbm, _, w1_ref, w2_ref, wkv_ref, sems):
    columns = wkv_ref.shape[2]
    mine = pl.ds(pl.multiple_of(chip_ref[0] * columns, HD), columns)
    loads = [
        pltpu.make_async_copy(w1_hbm, w1_ref, sems.at[0]),
        pltpu.make_async_copy(w2_hbm, w2_ref, sems.at[1]),
        pltpu.make_async_copy(wkv_hbm.at[:, :, mine], wkv_ref, sems.at[2]),
    ]
    for load in loads:
        load.start()
    for load in loads:
        load.wait()


def fetch(chip, w1, w2, w_kv, columns, after):
    shapes = [w1.shape, w2.shape, (w_kv.shape[0], w_kv.shape[1], columns)]
    return pl.pallas_call(
        fetch_kernel,
        in_specs=[SM, HB, HB, HB, AN],
        out_specs=[VM, VM, VM],
        out_shape=[jax.ShapeDtypeStruct(shape, BF16) for shape in shapes],
        scratch_shapes=[pltpu.SemaphoreType.DMA((3,))],
        compiler_params=params(16),
        cost_estimate=cost(0, 20 * w1.size),
        name="fetch",
    )(chip, in_hbm(w1), in_hbm(w2), in_hbm(w_kv), after)


def mlp_kernel(normed_ref, w1_ref, w2_ref, out_ref):
    hidden = jnp.dot(normed_ref[...], w1_ref[...], preferred_element_type=F32)
    inner = (0.5 * hidden * (1.0 + lax.erf(hidden * math.sqrt(0.5)))).astype(BF16)
    result = jnp.dot(inner, w2_ref[...], preferred_element_type=F32)
    out_ref[...] = result.astype(out_ref.dtype)


def mlp(normed, w1, w2, kept_as):
    return pl.pallas_call(
        mlp_kernel,
        in_specs=[VM, VM, VM],
        out_specs=VM,
        out_shape=jax.ShapeDtypeStruct(normed.shape, kept_as),
        compiler_params=params(14),
        cost_estimate=cost(4 * normed.size * w1.shape[1], 4 * w1.size, 2 * normed.size),
        name="mlp",
    )(normed, w1, w2)


def kv_kernel(start, core_ref, live_ref, keys_ref, gain_ref, own_ref, send_ref):
    half = keys_ref.shape[1]
    block = own_ref.shape[1] // 2
    core = core_ref[0]
    slot = lax.broadcasted_iota(jnp.int32, (half, 1), 0) + core * (KI // 2) + start
    live = slot < live_ref[0] * TILE_TOK
    gain = gain_ref[...].reshape(1, -1)

    def write(ref, which):
        for head in range(block // HD):
            at = pl.ds(pl.multiple_of(which * block + head * HD, HD), HD)
            keys = rms_norm(keys_ref[0, :, at], gain)
            ref[:, head * HD : (head + 1) * HD] = keys.astype(BF16)
            values = keys_ref[1, :, at]
            ref[:, block + head * HD : block + (head + 1) * HD] = jnp.where(
                live, values, DEAD
            ).astype(BF16)

    write(send_ref, 1 - core)
    write(own_ref, core)


def finish_kv(start, core, live_tiles, key_value, gain):
    _, half, columns = key_value.shape
    return pl.pallas_call(
        functools.partial(kv_kernel, start),
        in_specs=[SM, SM, VM, VM],
        out_specs=[VM, VM],
        out_shape=[jax.ShapeDtypeStruct((half, columns), BF16)] * 2,
        compiler_params=params(8),
        cost_estimate=cost(10 * key_value.size, 6 * key_value.size),
        name="finish_kv",
    )(core, live_tiles, key_value, gain)


def query_kernel(line, mask_ref, seq_ref, core_ref, text_ref, gain_ref, out_ref, flags_ref):
    kv_local, blocks, rows, _ = out_ref.shape
    group = rows // QB
    images = mask_ref.shape[0] // blocks
    lane = lax.broadcasted_iota(jnp.int32, (1, flags_ref.shape[1]), 1)
    for block in range(blocks):
        row = jnp.zeros_like(lane)
        seen = jnp.int32(0)
        for slot in range(images):
            image = slot
            if line:
                turned = (slot & 4) | (slot & 1) << 1 | (slot & 2) >> 1
                image = seq_ref[0] ^ jnp.where(core_ref[0] == 0, slot, turned)
            flag = mask_ref[block * images + image]
            row = jnp.where(lane == slot, flag, row)
            seen = seen + flag
        flags_ref[block : block + 1, :] = row
        flags_ref[blocks + block : blocks + block + 1, :] = jnp.zeros_like(lane) + seen
    gain = gain_ref[...].reshape(1, -1)
    for head in range(kv_local):
        for block in range(blocks):
            for member in range(group):
                at = (head * group + member) * HD
                part = text_ref[block * QB : (block + 1) * QB, at : at + HD].astype(F32)
                out_ref[head, block, member * QB : (member + 1) * QB, :] = (
                    rms_norm(part, gain) * (1.0 / math.sqrt(HD))
                ).astype(BF16)


def norm_queries(line, mask, seq, core, text, gain, kv_local):
    rows, columns = text.shape
    group = columns // HD // kv_local
    blocks, images = mask.shape
    lanes = -(-images // 128) * 128
    return pl.pallas_call(
        functools.partial(query_kernel, line),
        in_specs=[SM, SM, SM, VM, VM],
        out_specs=[VM, VM],
        out_shape=[
            jax.ShapeDtypeStruct((kv_local, rows // QB, group * QB, HD), BF16),
            jax.ShapeDtypeStruct((2 * blocks, lanes), jnp.int32),
        ],
        compiler_params=params(8),
        cost_estimate=cost(8 * rows * columns, 4 * rows * columns),
        name="norm_queries",
    )(mask.reshape(-1), seq, core, text, gain)


def cross_kernel(slots, images, first, last, flags_ref, q_ref, *refs):
    flat = sum(count for _, count in slots)
    kv_refs, refs = list(refs[:flat]), refs[flat:]
    refs = refs if first else refs[1:]
    kv_local, blocks, rows, _ = q_ref.shape
    group = rows // QB
    if last:
        out_hbm, acc, vals, out_ref, sems = refs
    else:
        acc, vals = refs

    def wanted(block, image):
        if isinstance(image, int):
            return flags_ref[block : block + 1, image : image + 1][0, 0] > 0
        row = flags_ref[block : block + 1, :]
        lane = lax.broadcasted_iota(jnp.int32, row.shape, 1)
        return jnp.max(jnp.where(lane == image, row, 0)) > 0

    def attend(block, head, member, chunks):
        at = slice(member * QB, (member + 1) * QB)
        keys = [kv[:, head * HD : (head + 1) * HD] for kv in chunks]
        keys = keys[0] if len(keys) == 1 else jnp.concatenate(keys, axis=0)
        sims = lax.dot_general(q_ref[head, block, at, :], keys, NT, preferred_element_type=F32)
        return jnp.dot(jnp.exp(sims).astype(BF16), vals[head], preferred_element_type=F32)

    def one_image(image, chunks, fresh):
        some = functools.reduce(jnp.logical_or, [wanted(block, image) for block in range(blocks)])

        @pl.when(some)
        def _():
            for head in range(kv_local):
                at = 0
                for kv in chunks:
                    values = kv[:, (kv_local + head) * HD : (kv_local + head + 1) * HD]
                    live = values < DEAD * 0.5
                    span = slice(at, at + values.shape[0])
                    vals[head, span, :HD] = jnp.where(live, values, jnp.zeros_like(values))
                    vals[head, span, HD:] = jnp.where(live, 1.0, 0.0).astype(BF16)
                    at += values.shape[0]

        for block in range(blocks):

            @pl.when(wanted(block, image))
            def _(block=block):
                for head in range(kv_local):
                    for member in range(group):
                        at = slice(member * QB, (member + 1) * QB)
                        more = attend(block, head, member, chunks)
                        acc[head, block, at, :] = more if fresh else acc[head, block, at, :] + more

            if fresh:

                @pl.when(jnp.logical_not(wanted(block, image)))
                def _(block=block):
                    acc[:, block] = jnp.zeros((kv_local, rows, 2 * HD), F32)

    if slots[0][0] is None:
        acc[...] = jnp.zeros_like(acc)

        @pl.loop(0, images)
        def _(image):
            one_image(image, [kv_refs[0].at[image]], False)
    else:
        for number, (bits, count) in enumerate(slots):
            one_image(bits, [kv_refs.pop(0) for _ in range(count)], first and number == 0)

    if not last:
        return
    span = group * HD
    copies = {}
    for block in range(blocks):
        seen = flags_ref[blocks + block : blocks + block + 1, :1][0, 0]
        for head in range(kv_local):
            rows_at = slice(block * QB, (block + 1) * QB)
            columns = slice(head * span, (head + 1) * span)

            @pl.when(seen > 0)
            def _(head=head, block=block, rows_at=rows_at):
                for member in range(group):
                    at = slice(member * QB, (member + 1) * QB)
                    column = (head * group + member) * HD
                    total = acc[head, block, at, :HD]
                    denom = acc[head, block, at, HD:]
                    inverse = pl.reciprocal(denom, approx=True)
                    inverse = inverse * (2.0 - denom * inverse)
                    out_ref[rows_at, column : column + HD] = (total * inverse).astype(BF16)

            @pl.when(seen == 0)
            def _(rows_at=rows_at, columns=columns):
                out_ref[rows_at, columns] = jnp.zeros((QB, span), BF16)

            copies[block, head] = pltpu.make_async_copy(
                out_ref.at[rows_at, columns], out_hbm.at[rows_at, columns], sems.at[block, head]
            )
            copies[block, head].start()
    for copy in copies.values():
        copy.wait()


def cross(images, flags, queries, slots, acc=None, last=True):
    kv_local, blocks, rows, _ = queries.shape
    flat = [chunk for _, chunks in slots for chunk in chunks]
    keys = sum(chunk.shape[-2] for chunk in slots[0][1])
    out = jax.ShapeDtypeStruct((blocks * QB, kv_local * (rows // QB) * HD), BF16)
    work = blocks * rows * sum(kv.size for kv in flat) // (2 * HD)
    sums = (kv_local, blocks, rows, 2 * HD)
    given = [] if acc is None else [acc]
    scratch = [pltpu.VMEM((kv_local, keys, 2 * HD), BF16)]
    if last:
        scratch += [pltpu.VMEM(out.shape, BF16), pltpu.SemaphoreType.DMA((blocks, kv_local))]
    result = pl.pallas_call(
        functools.partial(
            cross_kernel,
            [(bits, len(chunks)) for bits, chunks in slots],
            images,
            acc is None,
            last,
        ),
        in_specs=[VM, VM] + [VM] * len(flat + given),
        out_specs=[HB, VM] if last else [VM],
        out_shape=[out] * last + [jax.ShapeDtypeStruct(sums, F32)],
        scratch_shapes=scratch,
        input_output_aliases={2 + len(flat): int(last)} if given else {},
        compiler_params=params(14),
        cost_estimate=cost(4 * work * HD, 4 * queries.size, work),
        name="cross",
    )(flags, queries, *flat, *given)
    return result[0]


def swap_line(value, even, odd):
    heads = lax.axis_size("head")
    pairs = []
    for seq in range(lax.axis_size("seq")):
        for head in range(heads):
            other = seq ^ (odd if head % 2 else even)
            pairs.append((seq * heads + head, other * heads + head))
    return lax.ppermute(value, ("seq", "head"), pairs)


def tie(values, *after):
    return lax.optimization_barrier((tuple(values), after))[0]


def gather_line(blocks, attend):
    crossed = []

    def one(value):
        if len(crossed) > 1:
            value = tie((value,), crossed[-2])[0]
        crossed.append(swap_line(value, 1, 2))
        return crossed[-1]

    def two(value):
        return swap_line(value, 2, 1)

    def slots(*several):
        return [(bits, [got[bits] for got in images]) for bits in several]

    images = [{0: block, 4: swap_line(block, 4, 4)} for block in blocks]
    for got in images:
        got[1] = one(got[0])
    for got in images:
        got[2] = two(got[0])
    for got in images:
        got[6] = two(got[4])
        got[5] = one(got[4])
        got[3] = one(got[2])
    acc = attend(slots(0, 2, 1), None, False)
    images[1][5], acc = tie((images[1][5], acc))
    images[0][7] = one(images[0][6])
    images[1][7] = two(images[1][5])
    for several in ((4, 3, 5, 6), (7,)):
        acc = attend(slots(*several), acc, several == (7,))
    return acc


def per_device(
    vis_in,
    live_tiles,
    ln1_gain,
    w_qkv,
    w_out,
    ln2_gain,
    w_fc1,
    w_fc2,
    w_kv,
    k_gain,
    q_gain,
    text_queries,
    block_mask,
):
    head_count = lax.axis_size("head")
    head_index = lax.axis_index("head")
    core = head_index % 2
    core_arg = core.astype(jnp.int32).reshape(1)
    kv_local = KVH // head_count
    swap_core = functools.partial(
        lax.ppermute, axis_name="head", perm=[(i, i ^ 1) for i in range(head_count)]
    )

    def swap_chip(value, bit):
        return lax.ppermute(value, "head", [(i, i ^ bit) for i in range(head_count)])

    def sum_chips(value):
        bit = 2
        other = swap_chip(value, bit)
        while 2 * bit < head_count:
            bit *= 2
            value = (value.astype(F32) + other.astype(F32)).astype(BF16)
            other = swap_chip(value, bit)
        return value, other

    x = vis_in.reshape(vis_in.shape[0] * vis_in.shape[1], vis_in.shape[2])
    rows, width = x.shape
    half = rows // 2
    line = lax.axis_size("seq") == 8
    cuts = [0, half * FIRST // 128, half] if line else [0, half]
    chunks = [slice(at, end) for at, end in zip(cuts, cuts[1:])]
    chip_columns = 2 * kv_local * HD

    seq = lax.axis_index("seq").astype(jnp.int32).reshape(1)
    images = block_mask.shape[1]
    queries, flags = norm_queries(line, block_mask, seq, core_arg, text_queries, q_gain, kv_local)
    send, kept, own_x = encode(
        core_arg, live_tiles, x, ln1_gain, jnp.swapaxes(w_qkv, 1, 2), w_out
    )
    received = swap_core(send)
    chip_arg = (head_index // 2).astype(jnp.int32).reshape(1)
    first = (kept + received.astype(F32)).astype(BF16)
    w1, w2, w_chip = fetch(chip_arg, w_fc1, w_fc2, w_kv, chip_columns, first)
    first, second = sum_chips(first)
    resid, normed = mid(own_x, first, second, ln2_gain, w_chip, queries)
    other = swap_core(normed)
    keep = mlp(normed, w1, w2, F32)
    received = swap_core(mlp(other, w1, w2, BF16))
    sums = [(keep[at] + received[at].astype(F32)).astype(BF16) for at in chunks]
    sums = [sum_chips(value) for value in sums]
    blocks = []
    for at, (first, second) in zip(chunks, sums):
        second = tie((second,), blocks[-1] if blocks else sums[-1][0])[0]
        vision = (resid[at] + (first.astype(F32) + second.astype(F32))).astype(BF16)
        key_value = jnp.einsum("rc,cjd->jrd", vision, w_chip, preferred_element_type=F32)
        own, send = finish_kv(at.start, core_arg, live_tiles, key_value, k_gain)
        blocks.append(jnp.concatenate([own, swap_core(send)], axis=0))

    if not line:
        stacked = lax.all_gather(jnp.concatenate(blocks, axis=0), "seq", axis=0)
        return cross(images, flags, queries, [(None, [stacked])])
    return gather_line(blocks, functools.partial(cross, images, flags, queries))


def solution(mesh):
    placed = (
        P("seq", None, None),
        P("seq"),
        P(),
        P(None, None, "head"),
        P("head", None),
        P(),
        P(None, "head"),
        P("head", None),
        P(),
        P(),
        P(),
        P("seq", "head"),
        P("seq", None),
    )
    return jax.shard_map(
        per_device, mesh=mesh, in_specs=placed, out_specs=P("seq", "head"), check_vma=False
    )
```

```python
import functools
import math

import jax
import jax.numpy as jnp
from jax import lax
from jax.experimental import pallas as pl
from jax.experimental.pallas import tpu as pltpu
from jax.sharding import PartitionSpec as P

KVH = 8
HD = 128
TILE_TOK = 64
QB = 128
VHD = 80
KI = 256
DEAD = 1e30
FIRST = 64
EARLY = [[0], [2, 1]]
LATE = [[4, 3], [5, 6], [7]]
F32 = jnp.float32
BF16 = jnp.bfloat16

NT = (((1,), (1,)), ((), ()))
VM = pl.BlockSpec(memory_space=pltpu.VMEM)
SM = pl.BlockSpec(memory_space=pltpu.SMEM)
HB = pl.BlockSpec(memory_space=pltpu.HBM)
AN = pl.BlockSpec(memory_space=pl.ANY)


def params(mib):
    return pltpu.CompilerParams(vmem_limit_bytes=mib * 1024 * 1024)


def in_hbm(value):
    return pltpu.with_memory_space_constraint(value, pltpu.HBM)


def cost(flops, size, transcendentals=0):
    return pl.CostEstimate(flops=flops, bytes_accessed=size, transcendentals=transcendentals)


def layer_norm(values, gain):
    center = values - jnp.mean(values, axis=-1, keepdims=True)
    spread = jnp.mean(center * center, axis=-1, keepdims=True)
    return center * (1.0 / jnp.sqrt(spread + 1e-05)) * gain


def rms_norm(values, gain):
    square = jnp.mean(values * values, axis=-1, keepdims=True)
    return values * (1.0 / jnp.sqrt(square + 1e-05)) * gain


def encode_kernel(
    core_ref,
    live_ref,
    gain_hbm,
    x_hbm,
    wqkv_hbm,
    wout_hbm,
    send_ref,
    keep_ref,
    own_ref,
    gain_ref,
    x_ref,
    wqkv_ref,
    wout_ref,
    mixed_ref,
    sems,
):
    loads = [pltpu.make_async_copy(x_hbm, x_ref, sems.at[0])]
    loads.append(pltpu.make_async_copy(wqkv_hbm, wqkv_ref, sems.at[1]))
    loads.append(pltpu.make_async_copy(wout_hbm, wout_ref, sems.at[2]))
    loads.append(pltpu.make_async_copy(gain_hbm, gain_ref, sems.at[3]))
    for load in loads:
        load.start()
    rows, width = mixed_ref.shape
    half = rows // 2
    core = core_ref[0]
    own_rows = pl.ds(pl.multiple_of(core * half, half), half)
    other_rows = pl.ds(pl.multiple_of((1 - core) * half, half), half)

    loads[0].wait()
    loads[3].wait()
    own_ref[...] = x_ref[own_rows, :]
    normed = layer_norm(x_ref[...].astype(F32), gain_ref[...].reshape(1, -1)).astype(BF16)
    loads[1].wait()
    weights = wqkv_ref[...].reshape(3 * width, x_ref.shape[1])
    qkv = lax.dot_general(normed, weights, NT, preferred_element_type=F32).astype(BF16)
    q, k, v = [qkv[:, j * width : (j + 1) * width] for j in range(3)]
    lane = lax.broadcasted_iota(jnp.int32, (1, width), 1)
    slot = lax.broadcasted_iota(jnp.int32, (1, rows), 1)
    live = jnp.where(slot < live_ref[0] * TILE_TOK, 1.0, 0.0).astype(F32)
    zero = jnp.zeros_like(q)
    mixed = jnp.zeros((rows, width), F32)
    for head in range(width // VHD):
        own = (lane >= head * VHD) & (lane < (head + 1) * VHD)
        scores = lax.dot_general(jnp.where(own, q, zero), k, NT, preferred_element_type=F32)
        expo = jnp.exp(scores * (1.0 / math.sqrt(VHD))) * live
        probs = (expo * (1.0 / jnp.sum(expo, axis=-1, keepdims=True))).astype(BF16)
        mixed = mixed + jnp.dot(probs, jnp.where(own, v, zero), preferred_element_type=F32)
    mixed_ref[...] = mixed.astype(BF16)
    loads[2].wait()
    send_ref[...] = jnp.dot(
        mixed_ref[other_rows, :], wout_ref[...], preferred_element_type=F32
    ).astype(BF16)
    keep_ref[...] = jnp.dot(mixed_ref[own_rows, :], wout_ref[...], preferred_element_type=F32)


def encode(core, live_tiles, x, gain, w_qkv_t, w_out):
    rows, width = x.shape
    own = w_out.shape[0]
    return pl.pallas_call(
        encode_kernel,
        in_specs=[SM, SM, HB, HB, HB, HB],
        out_specs=[VM, VM, VM],
        out_shape=[
            jax.ShapeDtypeStruct((rows // 2, width), BF16),
            jax.ShapeDtypeStruct((rows // 2, width), F32),
            jax.ShapeDtypeStruct((rows // 2, width), BF16),
        ],
        scratch_shapes=[
            pltpu.VMEM(gain.shape, F32),
            pltpu.VMEM(x.shape, BF16),
            pltpu.VMEM(w_qkv_t.shape, BF16),
            pltpu.VMEM(w_out.shape, BF16),
            pltpu.VMEM((rows, own), BF16),
            pltpu.SemaphoreType.DMA((4,)),
        ],
        compiler_params=params(12),
        cost_estimate=cost(2 * rows * width * 4 * own, 8 * width * own, rows * rows * own // VHD),
        name="encode",
    )(core, live_tiles, in_hbm(gain), in_hbm(x), in_hbm(w_qkv_t), in_hbm(w_out))


def mid_kernel(x_ref, first_ref, second_ref, gain_ref, _, __, resid_ref, normed_ref):
    resid = x_ref[...].astype(F32) + (first_ref[...].astype(F32) + second_ref[...].astype(F32))
    resid_ref[...] = resid
    normed_ref[...] = layer_norm(resid, gain_ref[...].reshape(1, -1)).astype(BF16)


def mid(x, first, second, gain, *after):
    half, width = first.shape
    return pl.pallas_call(
        mid_kernel,
        in_specs=[VM, VM, VM, VM, AN, AN],
        out_specs=[VM, VM],
        out_shape=[
            jax.ShapeDtypeStruct((half, width), F32),
            jax.ShapeDtypeStruct((half, width), BF16),
        ],
        compiler_params=params(8),
        cost_estimate=cost(10 * half * width, 14 * half * width),
        name="mid",
    )(x, first, second, gain, *after)


def fetch_kernel(chip_ref, w1_hbm, w2_hbm, wkv_hbm, _, w1_ref, w2_ref, wkv_ref, sems):
    columns = wkv_ref.shape[2]
    mine = pl.ds(pl.multiple_of(chip_ref[0] * columns, HD), columns)
    loads = [
        pltpu.make_async_copy(w1_hbm, w1_ref, sems.at[0]),
        pltpu.make_async_copy(w2_hbm, w2_ref, sems.at[1]),
        pltpu.make_async_copy(wkv_hbm.at[:, :, mine], wkv_ref, sems.at[2]),
    ]
    for load in loads:
        load.start()
    for load in loads:
        load.wait()


def fetch(chip, w1, w2, w_kv, columns, after):
    shapes = [w1.shape, w2.shape, (w_kv.shape[0], w_kv.shape[1], columns)]
    return pl.pallas_call(
        fetch_kernel,
        in_specs=[SM, HB, HB, HB, AN],
        out_specs=[VM, VM, VM],
        out_shape=[jax.ShapeDtypeStruct(shape, BF16) for shape in shapes],
        scratch_shapes=[pltpu.SemaphoreType.DMA((3,))],
        compiler_params=params(16),
        cost_estimate=cost(0, 20 * w1.size),
        name="fetch",
    )(chip, in_hbm(w1), in_hbm(w2), in_hbm(w_kv), after)


def mlp_kernel(normed_ref, w1_ref, w2_ref, out_ref):
    hidden = jnp.dot(normed_ref[...], w1_ref[...], preferred_element_type=F32)
    inner = (0.5 * hidden * (1.0 + lax.erf(hidden * math.sqrt(0.5)))).astype(BF16)
    result = jnp.dot(inner, w2_ref[...], preferred_element_type=F32)
    out_ref[...] = result.astype(out_ref.dtype)


def mlp(normed, w1, w2, kept_as):
    return pl.pallas_call(
        mlp_kernel,
        in_specs=[VM, VM, VM],
        out_specs=VM,
        out_shape=jax.ShapeDtypeStruct(normed.shape, kept_as),
        compiler_params=params(14),
        cost_estimate=cost(4 * normed.size * w1.shape[1], 4 * w1.size, 2 * normed.size),
        name="mlp",
    )(normed, w1, w2)


def kv_kernel(start, core_ref, live_ref, keys_ref, gain_ref, own_ref, send_ref):
    half = keys_ref.shape[1]
    block = own_ref.shape[1] // 2
    core = core_ref[0]
    slot = lax.broadcasted_iota(jnp.int32, (half, 1), 0) + core * (KI // 2) + start
    live = slot < live_ref[0] * TILE_TOK
    gain = gain_ref[...].reshape(1, -1)

    def write(ref, which):
        for head in range(block // HD):
            at = pl.ds(pl.multiple_of(which * block + head * HD, HD), HD)
            keys = rms_norm(keys_ref[0, :, at], gain)
            ref[:, head * HD : (head + 1) * HD] = keys.astype(BF16)
            values = keys_ref[1, :, at]
            ref[:, block + head * HD : block + (head + 1) * HD] = jnp.where(
                live, values, DEAD
            ).astype(BF16)

    write(send_ref, 1 - core)
    write(own_ref, core)


def finish_kv(start, core, live_tiles, key_value, gain):
    _, half, columns = key_value.shape
    return pl.pallas_call(
        functools.partial(kv_kernel, start),
        in_specs=[SM, SM, VM, VM],
        out_specs=[VM, VM],
        out_shape=[jax.ShapeDtypeStruct((half, columns), BF16)] * 2,
        compiler_params=params(8),
        cost_estimate=cost(10 * key_value.size, 6 * key_value.size),
        name="finish_kv",
    )(core, live_tiles, key_value, gain)


def query_kernel(line, mask_ref, seq_ref, core_ref, text_ref, gain_ref, out_ref, flags_ref):
    kv_local, blocks, rows, _ = out_ref.shape
    group = rows // QB
    images = mask_ref.shape[0] // blocks
    lane = lax.broadcasted_iota(jnp.int32, (1, flags_ref.shape[1]), 1)
    for block in range(blocks):
        row = jnp.zeros_like(lane)
        seen = jnp.int32(0)
        for slot in range(images):
            image = slot
            if line:
                turned = (slot & 4) | (slot & 1) << 1 | (slot & 2) >> 1
                image = seq_ref[0] ^ jnp.where(core_ref[0] == 0, slot, turned)
            flag = mask_ref[block * images + image]
            row = jnp.where(lane == slot, flag, row)
            seen = seen + flag
        flags_ref[block : block + 1, :] = row
        flags_ref[blocks + block : blocks + block + 1, :] = jnp.zeros_like(lane) + seen
    gain = gain_ref[...].reshape(1, -1)
    for head in range(kv_local):
        for block in range(blocks):
            for member in range(group):
                at = (head * group + member) * HD
                part = text_ref[block * QB : (block + 1) * QB, at : at + HD].astype(F32)
                out_ref[head, block, member * QB : (member + 1) * QB, :] = (
                    rms_norm(part, gain) * (1.0 / math.sqrt(HD))
                ).astype(BF16)


def norm_queries(line, mask, seq, core, text, gain, kv_local):
    rows, columns = text.shape
    group = columns // HD // kv_local
    blocks, images = mask.shape
    lanes = -(-images // 128) * 128
    return pl.pallas_call(
        functools.partial(query_kernel, line),
        in_specs=[SM, SM, SM, VM, VM],
        out_specs=[VM, VM],
        out_shape=[
            jax.ShapeDtypeStruct((kv_local, rows // QB, group * QB, HD), BF16),
            jax.ShapeDtypeStruct((2 * blocks, lanes), jnp.int32),
        ],
        compiler_params=params(8),
        cost_estimate=cost(8 * rows * columns, 4 * rows * columns),
        name="norm_queries",
    )(mask.reshape(-1), seq, core, text, gain)


def cross_kernel(slots, images, first, last, flags_ref, q_ref, *refs):
    flat = sum(count for _, count in slots)
    kv_refs, refs = list(refs[:flat]), refs[flat:]
    refs = refs if first else refs[1:]
    kv_local, blocks, rows, _ = q_ref.shape
    group = rows // QB
    if last:
        out_hbm, acc, vals, out_ref, sems = refs
    else:
        acc, vals = refs

    def wanted(block, image):
        if isinstance(image, int):
            return flags_ref[block : block + 1, image : image + 1][0, 0] > 0
        row = flags_ref[block : block + 1, :]
        lane = lax.broadcasted_iota(jnp.int32, row.shape, 1)
        return jnp.max(jnp.where(lane == image, row, 0)) > 0

    def attend(block, head, member, chunks):
        at = slice(member * QB, (member + 1) * QB)
        keys = [kv[:, head * HD : (head + 1) * HD] for kv in chunks]
        keys = keys[0] if len(keys) == 1 else jnp.concatenate(keys, axis=0)
        sims = lax.dot_general(q_ref[head, block, at, :], keys, NT, preferred_element_type=F32)
        return jnp.dot(jnp.exp(sims).astype(BF16), vals[head], preferred_element_type=F32)

    def one_image(image, chunks, fresh):
        some = functools.reduce(jnp.logical_or, [wanted(block, image) for block in range(blocks)])

        @pl.when(some)
        def _():
            for head in range(kv_local):
                at = 0
                for kv in chunks:
                    values = kv[:, (kv_local + head) * HD : (kv_local + head + 1) * HD]
                    live = values < DEAD * 0.5
                    span = slice(at, at + values.shape[0])
                    vals[head, span, :HD] = jnp.where(live, values, jnp.zeros_like(values))
                    vals[head, span, HD:] = jnp.where(live, 1.0, 0.0).astype(BF16)
                    at += values.shape[0]

        for block in range(blocks):

            @pl.when(wanted(block, image))
            def _(block=block):
                for head in range(kv_local):
                    for member in range(group):
                        at = slice(member * QB, (member + 1) * QB)
                        more = attend(block, head, member, chunks)
                        acc[head, block, at, :] = more if fresh else acc[head, block, at, :] + more

            if fresh:

                @pl.when(jnp.logical_not(wanted(block, image)))
                def _(block=block):
                    acc[:, block] = jnp.zeros((kv_local, rows, 2 * HD), F32)

    if slots[0][0] is None:
        acc[...] = jnp.zeros_like(acc)

        @pl.loop(0, images)
        def _(image):
            one_image(image, [kv_refs[0].at[image]], False)
    else:
        for number, (bits, count) in enumerate(slots):
            one_image(bits, [kv_refs.pop(0) for _ in range(count)], first and number == 0)

    if not last:
        return
    span = group * HD
    copies = {}
    for block in range(blocks):
        seen = flags_ref[blocks + block : blocks + block + 1, :1][0, 0]
        for head in range(kv_local):
            rows_at = slice(block * QB, (block + 1) * QB)
            columns = slice(head * span, (head + 1) * span)

            @pl.when(seen > 0)
            def _(head=head, block=block, rows_at=rows_at):
                for member in range(group):
                    at = slice(member * QB, (member + 1) * QB)
                    column = (head * group + member) * HD
                    total = acc[head, block, at, :HD]
                    denom = acc[head, block, at, HD:]
                    inverse = pl.reciprocal(denom, approx=True)
                    inverse = inverse * (2.0 - denom * inverse)
                    out_ref[rows_at, column : column + HD] = (total * inverse).astype(BF16)

            @pl.when(seen == 0)
            def _(rows_at=rows_at, columns=columns):
                out_ref[rows_at, columns] = jnp.zeros((QB, span), BF16)

            copies[block, head] = pltpu.make_async_copy(
                out_ref.at[rows_at, columns], out_hbm.at[rows_at, columns], sems.at[block, head]
            )
            copies[block, head].start()
    for copy in copies.values():
        copy.wait()


def cross(images, flags, queries, slots, acc=None, last=True):
    kv_local, blocks, rows, _ = queries.shape
    flat = [chunk for _, chunks in slots for chunk in chunks]
    keys = sum(chunk.shape[-2] for chunk in slots[0][1])
    out = jax.ShapeDtypeStruct((blocks * QB, kv_local * (rows // QB) * HD), BF16)
    work = blocks * rows * sum(kv.size for kv in flat) // (2 * HD)
    sums = (kv_local, blocks, rows, 2 * HD)
    given = [] if acc is None else [acc]
    scratch = [pltpu.VMEM((kv_local, keys, 2 * HD), BF16)]
    if last:
        scratch += [pltpu.VMEM(out.shape, BF16), pltpu.SemaphoreType.DMA((blocks, kv_local))]
    result = pl.pallas_call(
        functools.partial(
            cross_kernel,
            [(bits, len(chunks)) for bits, chunks in slots],
            images,
            acc is None,
            last,
        ),
        in_specs=[VM, VM] + [VM] * len(flat + given),
        out_specs=[HB, VM] if last else [VM],
        out_shape=[out] * last + [jax.ShapeDtypeStruct(sums, F32)],
        scratch_shapes=scratch,
        input_output_aliases={2 + len(flat): int(last)} if given else {},
        compiler_params=params(14),
        cost_estimate=cost(4 * work * HD, 4 * queries.size, work),
        name="cross",
    )(flags, queries, *flat, *given)
    return result[0]


def swap_line(value, even, odd):
    heads = lax.axis_size("head")
    pairs = []
    for seq in range(lax.axis_size("seq")):
        for head in range(heads):
            other = seq ^ (odd if head % 2 else even)
            pairs.append((seq * heads + head, other * heads + head))
    return lax.ppermute(value, ("seq", "head"), pairs)


def tie(values, *after):
    return lax.optimization_barrier((tuple(values), after))[0]


def gather_line(blocks, attend):
    crossed = []

    def one(value):
        if len(crossed) > 1:
            value = tie((value,), crossed[-2])[0]
        crossed.append(swap_line(value, 1, 2))
        return crossed[-1]

    def two(value):
        return swap_line(value, 2, 1)

    def slots(*several):
        return [(bits, [got[bits] for got in images]) for bits in several]

    images = [{0: block, 4: swap_line(block, 4, 4)} for block in blocks]
    for got in images:
        got[1] = one(got[0])
    for got in images:
        got[2] = two(got[0])
    for got in images:
        got[6] = two(got[4])
        got[5] = one(got[4])
        got[3] = one(got[2])
    acc = attend(slots(0, 2, 1), None, False)
    images[1][5], acc = tie((images[1][5], acc))
    images[0][7] = two(images[0][5])
    images[1][7] = two(images[1][5])
    for several in ((4, 3, 5, 6), (7,)):
        acc = attend(slots(*several), acc, several == (7,))
    return acc


def per_device(
    vis_in,
    live_tiles,
    ln1_gain,
    w_qkv,
    w_out,
    ln2_gain,
    w_fc1,
    w_fc2,
    w_kv,
    k_gain,
    q_gain,
    text_queries,
    block_mask,
):
    head_count = lax.axis_size("head")
    head_index = lax.axis_index("head")
    core = head_index % 2
    core_arg = core.astype(jnp.int32).reshape(1)
    kv_local = KVH // head_count
    swap_core = functools.partial(
        lax.ppermute, axis_name="head", perm=[(i, i ^ 1) for i in range(head_count)]
    )

    def swap_chip(value, bit):
        return lax.ppermute(value, "head", [(i, i ^ bit) for i in range(head_count)])

    def sum_chips(value):
        bit = 2
        other = swap_chip(value, bit)
        while 2 * bit < head_count:
            bit *= 2
            value = (value.astype(F32) + other.astype(F32)).astype(BF16)
            other = swap_chip(value, bit)
        return value, other

    x = vis_in.reshape(vis_in.shape[0] * vis_in.shape[1], vis_in.shape[2])
    rows, width = x.shape
    half = rows // 2
    line = lax.axis_size("seq") == 8
    cuts = [0, half * FIRST // 128, half] if line else [0, half]
    chunks = [slice(at, end) for at, end in zip(cuts, cuts[1:])]
    chip_columns = 2 * kv_local * HD

    seq = lax.axis_index("seq").astype(jnp.int32).reshape(1)
    images = block_mask.shape[1]
    queries, flags = norm_queries(line, block_mask, seq, core_arg, text_queries, q_gain, kv_local)
    send, kept, own_x = encode(
        core_arg, live_tiles, x, ln1_gain, jnp.swapaxes(w_qkv, 1, 2), w_out
    )
    received = swap_core(send)
    chip_arg = (head_index // 2).astype(jnp.int32).reshape(1)
    first = (kept + received.astype(F32)).astype(BF16)
    w1, w2, w_chip = fetch(chip_arg, w_fc1, w_fc2, w_kv, chip_columns, first)
    first, second = sum_chips(first)
    resid, normed = mid(own_x, first, second, ln2_gain, w_chip, queries)
    other = swap_core(normed)
    keep = mlp(normed, w1, w2, F32)
    received = swap_core(mlp(other, w1, w2, BF16))
    sums = [(keep[at] + received[at].astype(F32)).astype(BF16) for at in chunks]
    sums = [sum_chips(value) for value in sums]
    blocks = []
    for at, (first, second) in zip(chunks, sums):
        second = tie((second,), blocks[-1] if blocks else sums[-1][0])[0]
        vision = (resid[at] + (first.astype(F32) + second.astype(F32))).astype(BF16)
        key_value = jnp.einsum("rc,cjd->jrd", vision, w_chip, preferred_element_type=F32)
        own, send = finish_kv(at.start, core_arg, live_tiles, key_value, k_gain)
        blocks.append(jnp.concatenate([own, swap_core(send)], axis=0))

    if not line:
        stacked = lax.all_gather(jnp.concatenate(blocks, axis=0), "seq", axis=0)
        return cross(images, flags, queries, [(None, [stacked])])
    return gather_line(blocks, functools.partial(cross, images, flags, queries))


def solution(mesh):
    placed = (
        P("seq", None, None),
        P("seq"),
        P(),
        P(None, None, "head"),
        P("head", None),
        P(),
        P(None, "head"),
        P("head", None),
        P(),
        P(),
        P(),
        P("seq", "head"),
        P("seq", None),
    )
    return jax.shard_map(
        per_device, mesh=mesh, in_specs=placed, out_specs=P("seq", "head"), check_vma=False
    )
```
